768 devices in a mesh: row: 16 (over y, core), col: 12 (over z), layer: 4 (over x).
Axes of the slice: x: 4, y: 8, z: 12, core: 2. Of those that a mesh axis runs over, the one named last changes fastest.
Arguments:
- left_blocks: bfloat16 [16, 12, 4, 2, 64, 64], P('row', 'col', 'layer')
- left_coords: int32 [16, 12, 4, 2, 2], P('row', 'col', 'layer'), may hold values from 0 to 383, as said below
- right_blocks: bfloat16 [16, 12, 4, 32, 64, 64], P('row', 'col', 'layer')
- right_coords: int32 [16, 12, 4, 32, 2], P('row', 'col', 'layer'), may hold values from 0 to 383, as said below
Outputs:
- product: float32 [16, 64, 384, 64], P('row', None, ('col', 'layer'))
The draws below stay inside these ranges and needn't reach their ends.
Inputs may be any that keep to these rules, and one draw needn't show every extreme that they name: `left_coords`: slot s of grid position (r, c, l) holds block row r and an inner index in the l-th quarter of 384, within its c-th of 12 equal pieces. Used slots of one device name distinct blocks; unused slots repeat the coordinates of slot 0 and hold zero blocks. At least half of the slots of every device are used, and all of them on some device. `right_coords`: slot s of grid position (r, c, l) holds an inner index in the l-th quarter of 384, within its r-th of 16 equal pieces, and a block column in c * 32 to (c + 1) * 32 - 1. Used slots of one device name distinct blocks; unused slots repeat the coordinates of slot 0 and hold zero blocks. At least half of the slots of every device are used, and all of them on some device.
All inputs are finite; a program needn't handle non-finite values.
Results may differ from the reference program's by a relative error of at most 0.011.
Values may be sent and summed in bfloat16 or wider, within the bound.
No kernel may reach another device: no remote copies, remote signals or barrier semaphores. Data moves between devices by JAX's collectives and lax.ppermute only.
A program may use at most 128 MiB of HBM per device.

```python
import jax
import jax.numpy as jnp
from jax import lax

BS = 64
NB = 384
MB = 1
NP = 32
NA = 2
NBAND = 16
N_ROW = 16
N_COL = 12
N_LAYER = 4


def device_grid():
    index = jnp.arange(N_ROW * N_COL * N_LAYER)
    return (index // (N_COL * N_LAYER), index // N_LAYER % N_COL, index % N_LAYER)


def slot_layout(key, slots, positions):
    total = N_ROW * N_COL * N_LAYER

    def one(index):
        local = jax.random.fold_in(key, index)
        order = jax.random.permutation(local, positions)[:slots]
        used = jax.random.randint(jax.random.fold_in(local, 7), (), (slots + 1) // 2, slots + 1)
        return (order, used)
    orders, used = jax.vmap(one)(jnp.arange(total))
    fullest = jax.random.randint(jax.random.fold_in(key, 5), (), 0, total)
    used = jnp.where(jnp.arange(total) == fullest, slots, used)
    live = jnp.arange(slots)[None, :] < used[:, None]
    orders = jnp.where(live, orders, orders[:, :1])
    return (orders, live)


def left_layout(key):
    key = jax.random.fold_in(key, 101)
    width = NB // N_LAYER // N_COL
    orders, live = slot_layout(key, NA, MB * width)
    row_at, col_at, layer_at = device_grid()
    rows = row_at[:, None] * MB + orders // width
    inner = layer_at[:, None] * (NB // N_LAYER) + col_at[:, None] * width + orders % width
    coords = jnp.stack([rows, inner], -1).astype(jnp.int32)
    return (coords.reshape(N_ROW, N_COL, N_LAYER, NA, 2), live.reshape(N_ROW, N_COL, N_LAYER, NA))


def right_layout(key):
    key = jax.random.fold_in(key, 202)
    width = NB // N_LAYER // N_ROW
    columns = NB // N_COL
    orders, live = slot_layout(key, NP, width * columns)
    row_at, col_at, layer_at = device_grid()
    inner = layer_at[:, None] * (NB // N_LAYER) + row_at[:, None] * width + orders // columns
    outer = col_at[:, None] * columns + orders % columns
    coords = jnp.stack([inner, outer], -1).astype(jnp.int32)
    return (coords.reshape(N_ROW, N_COL, N_LAYER, NP, 2), live.reshape(N_ROW, N_COL, N_LAYER, NP))


def draw_left_coords(key, part):
    return left_layout(key)[0]


def draw_right_coords(key, part):
    return right_layout(key)[0]


def draw_left_blocks(key, part):
    coords, live = left_layout(key)
    key = jax.random.fold_in(key, 3)
    shape = live.shape + (BS, BS)
    values = jax.random.normal(key, shape, jnp.float32)
    values = values * 0.2 * live[..., None, None].astype(jnp.float32)
    return values.astype(jnp.bfloat16)


def draw_right_blocks(key, part):
    coords, live = right_layout(key)
    key = jax.random.fold_in(key, 4)
    shape = live.shape + (BS, BS)
    values = jax.random.normal(key, shape, jnp.float32)
    values = values * 0.2 * live[..., None, None].astype(jnp.float32)
    return values.astype(jnp.bfloat16)


def setup_inputs(seed: int = 0) -> dict:
    arg_keys = jax.random.split(jax.random.key(seed), 5)
    return {
        "left_blocks": draw_left_blocks(jax.random.fold_in(arg_keys[4], 71), 0),
        "left_coords": draw_left_coords(jax.random.fold_in(arg_keys[4], 71), 0),
        "right_blocks": draw_right_blocks(jax.random.fold_in(arg_keys[4], 71), 0),
        "right_coords": draw_right_coords(jax.random.fold_in(arg_keys[4], 71), 0),
    }


def reference(left_blocks, left_coords, right_blocks, right_coords):
    flat_left = left_blocks.reshape(-1, BS, BS)
    flat_lc = left_coords.reshape(-1, 2)
    dense_left = jnp.zeros((NB, NBAND, BS, BS), jnp.bfloat16)
    dense_left = dense_left.at[flat_lc[:, 1], flat_lc[:, 0]].add(flat_left)
    group = NP * 4
    total = jnp.zeros((NB, NBAND, BS, BS), jnp.float32)
    for quarter in range(N_LAYER):
        blocks = right_blocks[:, :, quarter].reshape(-1, group, BS, BS)
        coords = right_coords[:, :, quarter].reshape(-1, group, 2)

        def step(acc, item):
            piece, where = item
            panels = dense_left[where[:, 0]].astype(jnp.float32)
            prod = jnp.einsum("gmab,gbc->gmac", panels, piece.astype(jnp.float32))
            return acc.at[where[:, 1]].add(prod), None

        acc, unused = lax.scan(step, jnp.zeros((NB, NBAND, BS, BS), jnp.float32), (blocks, coords))
        rounded = lax.optimization_barrier(acc.astype(jnp.bfloat16))
        total = total + rounded.astype(jnp.float32)
    return jnp.transpose(total, (1, 2, 0, 3))
```

```python
import functools

import jax
import jax.numpy as jnp
from jax import lax
from jax.experimental import pallas as pl
from jax.experimental.pallas import tpu as pltpu
from jax.sharding import Mesh
from jax.sharding import PartitionSpec as P

NB = 384
BS = 64
N_Y = 8
N_COL = 12
N_LAYER = 4
SLOTS = 32
PAIRS = SLOTS // 2
BODY = PAIRS * BS
MSG = BODY + 16
LMSG = BS + 16
INNER = 6
COLUMNS = NB // N_COL
PIECE = NB // N_LAYER // N_COL
DEPTH = INNER * BS
WIDTH = COLUMNS * BS
STEPS = (0, 1, 1, 2, 2, 3, 3, 4)
OTHER = (0, 0, 1, 0, 1, 0, 1, 0)


def multiply_kernel(own, other, *refs):
    blocks, (out, left, panel, swapped, total, where, places, sem) = refs[:8], refs[8:]
    y = lax.axis_index("y")
    core = lax.axis_index("core")
    for j in range(8):
        tail = blocks[j][BODY:MSG, :].astype(jnp.float32).astype(jnp.int32)
        where[2 * j : 2 * j + 2, :] = tail[0:2, :]
    copy = pltpu.make_async_copy(where, places, sem)
    copy.start()

    to = lax.broadcasted_iota(jnp.int32, (128, 128), 1)
    frm = lax.broadcasted_iota(jnp.int32, (128, 128), 0)
    swap = (to == (frm + BS) % 128).astype(jnp.bfloat16)
    lane = lax.broadcasted_iota(jnp.int32, (BS, 128), 1)
    upper = (lane >= BS).astype(jnp.float32)

    for src, at in ((own, core), (other, 1 - core)):
        rows = pl.ds(pl.multiple_of(at * BS, BS), BS)
        for c in range(N_COL):
            whole = src[c]
            turned = jnp.dot(whole, swap, preferred_element_type=jnp.float32)
            whole = whole.astype(jnp.float32)
            here, there = whole[:BS], turned[:BS]
            k_here, k_there = whole[BS : BS + 1], turned[BS : BS + 1]
            for g in range(PIECE // 2):
                want = upper + 2.0 * g
                value = jnp.where(k_here == want, here, 0.0) + jnp.where(k_there == want, there, 0.0)
                at_lane = (c * PIECE + 2 * g) * BS
                left[rows, at_lane : at_lane + 128] = value.astype(jnp.bfloat16)

    low = (lane < BS).astype(jnp.bfloat16)
    high = (lane >= BS).astype(jnp.bfloat16)
    copy.wait()
    for j in range(8):
        panel[...] = jnp.zeros_like(panel)
        swapped[...] = jnp.dot(
            blocks[j][:BODY, :], swap, preferred_element_type=jnp.float32
        ).astype(jnp.bfloat16)

        def place(p, carry):
            at = pl.ds(pl.multiple_of(p * BS, BS), BS)
            tile = blocks[j][at, :]
            turned = swapped[at, :]
            for half in range(2):
                k = places[2 * j, p + half * PAIRS]
                n = places[2 * j + 1, p + half * PAIRS]
                odd = n % 2
                value = jnp.where(odd == half, tile, turned) * jnp.where(odd == 1, high, low)
                rows = pl.ds(pl.multiple_of(k * BS, BS), BS)
                lanes = pl.ds(pl.multiple_of((n // 2) * 128, 128), 128)
                panel[rows, lanes] = panel[rows, lanes] + value
            return carry

        lax.fori_loop(0, PAIRS, place, 0)
        chip = lax.rem(y + N_Y + jnp.where(core == 0, -STEPS[j], STEPS[j]), N_Y)
        owner = chip * 2 + (1 - core if OTHER[j] else core)
        at = pl.ds(pl.multiple_of(owner * DEPTH, 128), DEPTH)
        part = jnp.dot(left[:, at], panel[...], preferred_element_type=jnp.float32)
        total[...] = part if j == 0 else total[...] + part
    share = WIDTH // N_LAYER
    for m in range(2):
        for s in range(N_LAYER):
            out[m * N_LAYER + s] = total[m * BS : (m + 1) * BS, s * share : (s + 1) * share].astype(
                jnp.bfloat16
            )


def multiply(own, other, blocks):
    vmem = pl.BlockSpec(memory_space=pltpu.VMEM)
    return pl.pallas_call(
        multiply_kernel,
        out_shape=jax.ShapeDtypeStruct((2 * N_LAYER, BS, WIDTH // N_LAYER), jnp.bfloat16),
        in_specs=[vmem] * 10,
        out_specs=vmem,
        scratch_shapes=[
            pltpu.VMEM((2 * BS, NB // N_LAYER * BS), jnp.bfloat16),
            pltpu.VMEM((DEPTH, WIDTH), jnp.bfloat16),
            pltpu.VMEM((BODY, 128), jnp.bfloat16),
            pltpu.VMEM((2 * BS, WIDTH), jnp.float32),
            pltpu.VMEM((16, 128), jnp.int32),
            pltpu.SMEM((16, 128), jnp.int32),
            pltpu.SemaphoreType.DMA,
        ],
        compiler_params=pltpu.CompilerParams(vmem_limit_bytes=40 * 1024 * 1024),
        cost_estimate=pl.CostEstimate(
            flops=2 * 128 * 3072 * 2048, bytes_accessed=4 << 20, transcendentals=0
        ),
    )(own, other, *blocks)


def shards(left_blocks, left_coords, right_blocks, right_coords):
    y = lax.axis_index("y")
    core = lax.axis_index("core")
    col = lax.axis_index("col")
    layer = lax.axis_index("layer")
    base = layer * (NB // N_LAYER)

    r = right_blocks.reshape(SLOTS, BS, BS)
    body = jnp.concatenate([r[:PAIRS], r[PAIRS:]], axis=-1).reshape(BODY, 128)
    rc = right_coords.reshape(SLOTS, 2)
    inner = rc[:, 0] - (base + (y * 2 + core) * INNER)
    column = rc[:, 1] - col * COLUMNS
    tail = jnp.stack([inner, column]).astype(jnp.bfloat16)
    tail = jnp.pad(tail, ((0, 14), (0, 128 - SLOTS)))
    mine = jnp.concatenate([body, tail], axis=0)

    b = left_blocks.reshape(2, BS, BS)
    at = (left_coords.reshape(2, 2)[:, 1] - (base + col * PIECE)).astype(jnp.bfloat16)
    at = jnp.broadcast_to(jnp.repeat(at, BS)[None, :], (16, 128))
    piece = jnp.concatenate([jnp.concatenate([b[0], b[1]], axis=-1), at], axis=0)

    ring = [((2 * i + c), ((2 * ((i + (1 if c == 0 else -1)) % N_Y)) + c)) for i in range(N_Y) for c in (0, 1)]
    cores = [(i, i ^ 1) for i in range(2 * N_Y)]
    axes = ("y", "core")

    a = lax.ppermute(mine, axes, ring)
    theirs = lax.ppermute(mine, axes, cores)
    pieces = lax.all_to_all(jnp.broadcast_to(piece[None], (N_COL, LMSG, 128)), "col", 0, 0)
    blocks = [mine, a]
    o = theirs
    for step in range(1, 4):
        o = lax.ppermute(o, axes, ring)
        blocks.append(o)
        a = lax.ppermute(a, axes, ring)
        blocks.append(a)
    pieces_other = lax.ppermute(pieces, axes, cores)
    part = multiply(pieces, pieces_other, blocks)
    parts = lax.all_to_all(part, ("core", "layer"), 0, 0)
    total = jnp.sum(parts.astype(jnp.float32), axis=0)
    return total.reshape(1, BS, COLUMNS // N_LAYER, BS)


def solution(mesh):
    grid = Mesh(mesh.devices.reshape(N_Y, 2, N_COL, N_LAYER), ("y", "core", "col", "layer"))
    row = ("y", "core")
    return jax.shard_map(
        shards,
        mesh=grid,
        in_specs=(
            P(row, "col", "layer", None, None, None),
            P(row, "col", "layer", None, None),
            P(row, "col", "layer", None, None, None),
            P(row, "col", "layer", None, None),
        ),
        out_specs=P(row, None, ("col", "layer"), None),
        check_vma=False,
    )
```

```python
import jax
import jax.numpy as jnp
from jax import lax
from jax.experimental import pallas as pl
from jax.experimental.pallas import tpu as pltpu
from jax.sharding import Mesh
from jax.sharding import PartitionSpec as P

NB = 384
BS = 64
N_Y = 8
N_COL = 12
N_LAYER = 4
SLOTS = 32
PAIRS = SLOTS // 2
BODY = PAIRS * BS
MSG = BODY + 16
LMSG = BS + 16
INNER = 6
COLUMNS = NB // N_COL
PIECE = NB // N_LAYER // N_COL
DEPTH = INNER * BS
WIDTH = COLUMNS * BS
STEPS = (0, 1, 1, 2, 2, 3, 3, 4)
OTHER = (0, 0, 1, 0, 1, 0, 1, 0)
EARLY_COST = 64 << 20
EARLY = 5


def pack_kernel(right, right_where, left, left_where, out, tail):
    y = lax.axis_index("y")
    core = lax.axis_index("core")
    col = lax.axis_index("col")
    base = lax.axis_index("layer") * (NB // N_LAYER)
    for p in range(PAIRS):
        out[p * BS : (p + 1) * BS, :] = jnp.concatenate([right[p], right[p + PAIRS]], axis=-1)
    tail[...] = jnp.zeros_like(tail)
    inner = right_where[0:1, :] - (base + (y * 2 + core) * INNER)
    column = right_where[1:2, :] - col * COLUMNS
    tail[0:1, 0:SLOTS] = inner.astype(jnp.float32)
    tail[1:2, 0:SLOTS] = column.astype(jnp.float32)
    out[BODY:MSG, :] = tail[...].astype(jnp.bfloat16)
    out[MSG : MSG + BS, :] = jnp.concatenate([left[0], left[1]], axis=-1)
    lane = lax.broadcasted_iota(jnp.int32, (16, 128), 1)
    first = jnp.broadcast_to(left_where[0:1, 1:2], (16, 128))
    second = jnp.broadcast_to(left_where[1:2, 1:2], (16, 128))
    at = jnp.where(lane < BS, first, second) - (base + col * PIECE)
    out[MSG + BS :, :] = at.astype(jnp.float32).astype(jnp.bfloat16)


def pack(right, right_where, left, left_where):
    vmem = pl.BlockSpec(memory_space=pltpu.VMEM)
    return pl.pallas_call(
        pack_kernel,
        out_shape=jax.ShapeDtypeStruct((MSG + LMSG, 128), jnp.bfloat16),
        in_specs=[vmem] * 4,
        out_specs=vmem,
        scratch_shapes=[pltpu.VMEM((16, 128), jnp.float32)],
        cost_estimate=pl.CostEstimate(flops=0, bytes_accessed=1 << 20, transcendentals=0),
    )(right, right_where, left, left_where)


def spread_kernel(mine, theirs, out):
    first = lax.broadcasted_iota(jnp.int32, (16, 128), 0) == 0
    tail = jnp.where(
        first, mine[MSG + BS :, :].astype(jnp.float32), theirs[MSG + BS :, :].astype(jnp.float32)
    ).astype(jnp.bfloat16)
    for c in range(N_COL):
        out[c, :BS, :] = mine[MSG : MSG + BS, :]
        out[c, BS : 2 * BS, :] = theirs[MSG : MSG + BS, :]
        out[c, 2 * BS :, :] = tail


def spread(mine, theirs):
    vmem = pl.BlockSpec(memory_space=pltpu.VMEM)
    return pl.pallas_call(
        spread_kernel,
        out_shape=jax.ShapeDtypeStruct((N_COL, 2 * BS + 16, 128), jnp.bfloat16),
        in_specs=[vmem, vmem],
        out_specs=vmem,
        cost_estimate=pl.CostEstimate(flops=0, bytes_accessed=1 << 20, transcendentals=0),
    )(mine, theirs)


def half_swap():
    to = lax.broadcasted_iota(jnp.int32, (128, 128), 1)
    frm = lax.broadcasted_iota(jnp.int32, (128, 128), 0)
    return (to == (frm + BS) % 128).astype(jnp.bfloat16)


def read_places(blocks, where, places, sem):
    for j, (ref, top) in enumerate(blocks):
        tail = ref[top + BODY : top + MSG, :].astype(jnp.float32).astype(jnp.int32)
        where[2 * j : 2 * j + 2, :] = tail[0:2, :]
    copy = pltpu.make_async_copy(where, places, sem)
    copy.start()
    return copy


def place_slots(blocks, first, panels, swapped, places):
    lane = lax.broadcasted_iota(jnp.int32, (BS, 128), 1)
    low = (lane < BS).astype(jnp.bfloat16)
    high = (lane >= BS).astype(jnp.bfloat16)

    def place(p, carry):
        for half in range(2):
            for i, (ref, top) in enumerate(blocks):
                k = places[2 * (first + i), p + half * PAIRS]
                n = places[2 * (first + i) + 1, p + half * PAIRS]
                odd = n & 1
                tile = ref[pl.ds(pl.multiple_of(top + p * BS, 16), BS), :]
                turned = swapped[i][pl.ds(pl.multiple_of(p * BS, BS), BS), :]
                value = jnp.where(odd == half, tile, turned) * jnp.where(odd == 1, high, low)
                rows = pl.ds(pl.multiple_of(k * BS, BS), BS)
                lanes = pl.ds(pl.multiple_of((n >> 1) * 128, 128), 128)
                panels[i][rows, lanes] = panels[i][rows, lanes] + value
        return carry

    lax.fori_loop(0, PAIRS, place, 0, unroll=2)


def clear_and_swap(blocks, panels, swapped):
    swap = half_swap()
    for i, (ref, top) in enumerate(blocks):
        panels[i][...] = jnp.zeros_like(panels[i])
        swapped[i][...] = jnp.dot(
            ref[top : top + BODY, :], swap, preferred_element_type=jnp.float32
        ).astype(jnp.bfloat16)


def early_kernel(mine, one, two, out, where, places, sem, sems, *scratch):
    panels, swapped = scratch[:EARLY], scratch[EARLY:]
    blocks = ((mine, 0), (one, 0), (one, MSG), (two, 0), (two, MSG))
    copy = read_places(blocks, where, places, sem)
    copies = [pltpu.make_async_copy(panels[j], out.at[j], sems.at[j]) for j in range(EARLY)]
    for lo, hi in ((0, 3), (3, EARLY)):
        clear_and_swap(blocks[lo:hi], panels[lo:hi], swapped[lo:hi])
        if lo == 0:
            copy.wait()
        place_slots(blocks[lo:hi], lo, panels[lo:hi], swapped[lo:hi], places)
        for j in range(lo, hi):
            copies[j].start()
    for c in copies:
        c.wait()


def early(mine, one, two):
    vmem = pl.BlockSpec(memory_space=pltpu.VMEM)
    return pl.pallas_call(
        early_kernel,
        out_shape=jax.ShapeDtypeStruct((EARLY, DEPTH, WIDTH), jnp.bfloat16),
        in_specs=[vmem] * 3,
        out_specs=pl.BlockSpec(memory_space=pl.ANY),
        scratch_shapes=[
            pltpu.VMEM((16, 128), jnp.int32),
            pltpu.SMEM((16, 128), jnp.int32),
            pltpu.SemaphoreType.DMA,
            pltpu.SemaphoreType.DMA((EARLY,)),
        ]
        + [pltpu.VMEM((DEPTH, WIDTH), jnp.bfloat16)] * EARLY
        + [pltpu.VMEM((BODY, 128), jnp.bfloat16)] * EARLY,
        compiler_params=pltpu.CompilerParams(vmem_limit_bytes=24 * 1024 * 1024),
        cost_estimate=pl.CostEstimate(flops=0, bytes_accessed=EARLY_COST, transcendentals=0),
    )(mine, one, two)


def multiply_kernel(pieces, ready, three, four, out, left, total, where, places, sem, sems, *scratch):
    panels, swapped = scratch[:8], scratch[8:]
    blocks = ((three, 0), (three, MSG), (four, 0))
    y = lax.axis_index("y")
    core = lax.axis_index("core")
    copies = [pltpu.make_async_copy(ready.at[j], panels[j], sems.at[j]) for j in range(EARLY)]
    for c in copies:
        c.start()
    copy = read_places(blocks, where, places, sem)

    swap = half_swap()
    lane = lax.broadcasted_iota(jnp.int32, (BS, 128), 1)
    upper = (lane >= BS).astype(jnp.float32)
    for m, at in ((0, core), (1, 1 - core)):
        rows = pl.ds(pl.multiple_of(at * BS, BS), BS)
        for c in range(N_COL):
            here = pieces[c, m * BS : (m + 1) * BS, :]
            marks = pieces[c, 2 * BS :, :]
            there = jnp.dot(here, swap, preferred_element_type=jnp.float32)
            k_there = jnp.dot(marks, swap, preferred_element_type=jnp.float32)[m : m + 1]
            here = here.astype(jnp.float32)
            k_here = marks.astype(jnp.float32)[m : m + 1]
            for g in range(PIECE // 2):
                want = upper + 2.0 * g
                value = jnp.where(k_here == want, here, 0.0) + jnp.where(k_there == want, there, 0.0)
                at_lane = (c * PIECE + 2 * g) * BS
                left[rows, at_lane : at_lane + 128] = value.astype(jnp.bfloat16)

    clear_and_swap(blocks, panels[EARLY:], swapped)
    copy.wait()
    place_slots(blocks, 0, panels[EARLY:], swapped, places)
    for j in range(8):
        if j < EARLY:
            copies[j].wait()
        chip = lax.rem(y + N_Y + jnp.where(core == 0, -STEPS[j], STEPS[j]), N_Y)
        owner = chip * 2 + (1 - core if OTHER[j] else core)
        at = pl.ds(pl.multiple_of(owner * DEPTH, 128), DEPTH)
        part = jnp.dot(left[:, at], panels[j][...], preferred_element_type=jnp.float32)
        total[...] = part if j == 0 else total[...] + part
    share = WIDTH // N_LAYER
    for m in range(2):
        for s in range(N_LAYER):
            out[m * N_LAYER + s] = total[m * BS : (m + 1) * BS, s * share : (s + 1) * share].astype(
                jnp.bfloat16
            )


def multiply(pieces, ready, three, four):
    vmem = pl.BlockSpec(memory_space=pltpu.VMEM)
    return pl.pallas_call(
        multiply_kernel,
        out_shape=jax.ShapeDtypeStruct((2 * N_LAYER, BS, WIDTH // N_LAYER), jnp.bfloat16),
        in_specs=[vmem, pl.BlockSpec(memory_space=pl.ANY), vmem, vmem],
        out_specs=vmem,
        scratch_shapes=[
            pltpu.VMEM((2 * BS, NB // N_LAYER * BS), jnp.bfloat16),
            pltpu.VMEM((2 * BS, WIDTH), jnp.float32),
            pltpu.VMEM((16, 128), jnp.int32),
            pltpu.SMEM((16, 128), jnp.int32),
            pltpu.SemaphoreType.DMA,
            pltpu.SemaphoreType.DMA((EARLY,)),
        ]
        + [pltpu.VMEM((DEPTH, WIDTH), jnp.bfloat16)] * 8
        + [pltpu.VMEM((BODY, 128), jnp.bfloat16)] * (8 - EARLY),
        compiler_params=pltpu.CompilerParams(vmem_limit_bytes=32 * 1024 * 1024),
        cost_estimate=pl.CostEstimate(
            flops=2 * 128 * 3072 * 2048, bytes_accessed=16 << 20, transcendentals=0
        ),
    )(pieces, ready, three, four)


def around(distance):
    return [
        (2 * i + c, 2 * ((i + (distance if c == 0 else -distance)) % N_Y) + c)
        for i in range(N_Y)
        for c in (0, 1)
    ]


def shards(left_blocks, left_coords, right_blocks, right_coords):
    axes = ("y", "core")
    mine = pack(
        right_blocks.reshape(SLOTS, BS, BS),
        right_coords.reshape(SLOTS, 2).T,
        left_blocks.reshape(2, BS, BS),
        left_coords.reshape(2, 2),
    )
    theirs = lax.ppermute(mine, axes, [(i, i ^ 1) for i in range(2 * N_Y)])
    both = jnp.concatenate([mine[:MSG], theirs[:MSG]], axis=0)
    one = lax.ppermute(both, axes, around(1))
    two = lax.ppermute(both, axes, around(2))
    pieces = lax.all_to_all(spread(mine, theirs), "col", 0, 0)
    three = lax.ppermute(two, axes, around(1))
    four = lax.ppermute(two[:MSG], axes, around(2))
    part = multiply(pieces, early(mine, one, two), three, four)
    parts = lax.all_to_all(part, ("core", "layer"), 0, 0)
    total = jnp.sum(parts.astype(jnp.float32), axis=0)
    return total.reshape(1, BS, COLUMNS // N_LAYER, BS)


def solution(mesh):
    grid = Mesh(mesh.devices.reshape(N_Y, 2, N_COL, N_LAYER), ("y", "core", "col", "layer"))
    row = ("y", "core")
    return jax.shard_map(
        shards,
        mesh=grid,
        in_specs=(
            P(row, "col", "layer", None, None, None),
            P(row, "col", "layer", None, None),
            P(row, "col", "layer", None, None, None),
            P(row, "col", "layer", None, None),
        ),
        out_specs=P(row, None, ("col", "layer"), None),
        check_vma=False,
    )
```

```python
import jax
import jax.numpy as jnp
from jax import lax
from jax.experimental import pallas as pl
from jax.experimental.pallas import tpu as pltpu
from jax.sharding import Mesh
from jax.sharding import PartitionSpec as P

NB = 384
BS = 64
N_YH = 4
N_COL = 12
N_LAYER = 4
SLOTS = 32
PAIRS = SLOTS // 2
BODY = PAIRS * BS
MSG = BODY + 16
LMSG = BS + 16
INNER = 6
COLUMNS = NB // N_COL
PIECE = NB // N_LAYER // N_COL
DEPTH = INNER * BS
WIDTH = COLUMNS * BS
GROUP = 4
WINDOW = 2 * PIECE * BS


def pack_kernel(right, right_where, left, left_where, out, piece, tail):
    y = lax.axis_index("yh") * 2 + lax.axis_index("yl")
    core = lax.axis_index("core")
    col = lax.axis_index("col")
    base = lax.axis_index("layer") * (NB // N_LAYER)
    for p in range(PAIRS):
        pair = jnp.concatenate([right[p], right[p + PAIRS]], axis=-1)
        for q in range(N_YH):
            out[q, p * BS : (p + 1) * BS, :] = pair
    tail[...] = jnp.zeros_like(tail)
    inner = right_where[0:1, :] - (base + (y * 2 + core) * INNER)
    column = right_where[1:2, :] - col * COLUMNS
    tail[0:1, 0:SLOTS] = inner.astype(jnp.float32)
    tail[1:2, 0:SLOTS] = column.astype(jnp.float32)
    for q in range(N_YH):
        out[q, BODY:MSG, :] = tail[...].astype(jnp.bfloat16)
    lane = lax.broadcasted_iota(jnp.int32, (16, 128), 1)
    first = jnp.broadcast_to(left_where[0:1, 1:2], (16, 128))
    second = jnp.broadcast_to(left_where[1:2, 1:2], (16, 128))
    at = jnp.where(lane < BS, first, second) - (base + col * PIECE)
    at = at.astype(jnp.float32).astype(jnp.bfloat16)
    pair = jnp.concatenate([left[0], left[1]], axis=-1)
    piece[:BS, :] = pair
    piece[BS:, :] = at


def pack(right, right_where, left, left_where):
    vmem = pl.BlockSpec(memory_space=pltpu.VMEM)
    return pl.pallas_call(
        pack_kernel,
        out_shape=(
            jax.ShapeDtypeStruct((N_YH, MSG, 128), jnp.bfloat16),
            jax.ShapeDtypeStruct((LMSG, 128), jnp.bfloat16),
        ),
        in_specs=[vmem] * 4,
        out_specs=(vmem, vmem),
        scratch_shapes=[pltpu.VMEM((16, 128), jnp.float32)],
        cost_estimate=pl.CostEstimate(flops=0, bytes_accessed=2 << 20, transcendentals=0),
    )(right, right_where, left, left_where)


def half_swap():
    to = lax.broadcasted_iota(jnp.int32, (128, 128), 1)
    frm = lax.broadcasted_iota(jnp.int32, (128, 128), 0)
    return (to == (frm + BS) % 128).astype(jnp.bfloat16)


def read_places(blocks, where, places, sem):
    for i, block in enumerate(blocks):
        tail = block[BODY:MSG, :].astype(jnp.float32).astype(jnp.int32)
        where[2 * i : 2 * i + 2, :] = tail[0:2, :]
    copy = pltpu.make_async_copy(where, places, sem)
    copy.start()
    return copy


def place_slots(blocks, first, panels, swapped, places):
    lane = lax.broadcasted_iota(jnp.int32, (BS, 128), 1)
    low = (lane < BS).astype(jnp.bfloat16)
    high = (lane >= BS).astype(jnp.bfloat16)

    def place(p, carry):
        at = pl.ds(pl.multiple_of(p * BS, BS), BS)
        for half in range(2):
            for i, block in enumerate(blocks):
                k = places[2 * (first + i), p + half * PAIRS]
                n = places[2 * (first + i) + 1, p + half * PAIRS]
                odd = n & 1
                value = jnp.where(odd == half, block[at, :], swapped[i][at, :])
                value = value * jnp.where(odd == 1, high, low)
                rows = pl.ds(pl.multiple_of(k * BS, BS), BS)
                lanes = pl.ds(pl.multiple_of((n >> 1) * 128, 128), 128)
                panels[i][rows, lanes] = panels[i][rows, lanes] + value
        return carry

    lax.fori_loop(0, PAIRS, place, 0, unroll=2)


def place_kernel(own, other, left_own, left_other, out, left, total, where, places, sem, *scratch):
    panels, swapped = scratch[:GROUP], scratch[GROUP:]
    yl = lax.axis_index("yl")
    core = lax.axis_index("core")
    blocks = [own.at[q] for q in range(N_YH)] + [other.at[q] for q in range(N_YH)]
    copy = read_places(blocks, where, places, sem)
    swap = half_swap()

    lane = lax.broadcasted_iota(jnp.int32, (BS, 128), 1)
    upper = (lane >= BS).astype(jnp.float32)
    for src, at in ((left_own, yl), (left_other, 1 - yl)):
        rows = pl.ds(pl.multiple_of(at * BS, BS), BS)
        for q in range(N_YH):
            for u in range(2):
                whole = src[3 * q + yl + u] if src is left_own else src[2 * q + u]
                there = jnp.dot(whole, swap, preferred_element_type=jnp.float32)
                here = whole.astype(jnp.float32)
                for g in range(PIECE // 2):
                    want = upper + 2.0 * g
                    value = jnp.where(here[BS : BS + 1] == want, here[:BS], 0.0)
                    value = value + jnp.where(there[BS : BS + 1] == want, there[:BS], 0.0)
                    at_lane = q * WINDOW + (u * PIECE + 2 * g) * BS
                    left[rows, at_lane : at_lane + 128] = value.astype(jnp.bfloat16)

    for j0 in range(0, 2 * N_YH, GROUP):
        now = blocks[j0 : j0 + GROUP]
        for i, block in enumerate(now):
            panels[i][...] = jnp.zeros_like(panels[i])
            swapped[i][...] = jnp.dot(
                block[:BODY, :], swap, preferred_element_type=jnp.float32
            ).astype(jnp.bfloat16)
        if j0 == 0:
            copy.wait()
        place_slots(now, j0, panels, swapped, places)
        for i in range(len(now)):
            j = j0 + i
            side = core if j < N_YH else 1 - core
            start = (j % N_YH) * WINDOW + yl * (4 * BS) + side * DEPTH
            at = pl.ds(pl.multiple_of(start, 128), DEPTH)
            part = jnp.dot(left[:, at], panels[i][...], preferred_element_type=jnp.float32)
            total[...] = part if j == 0 else total[...] + part
    share = WIDTH // N_LAYER
    for m in range(2):
        for s in range(N_LAYER):
            out[m * N_LAYER + s] = total[m * BS : (m + 1) * BS, s * share : (s + 1) * share].astype(
                jnp.bfloat16
            )


def multiply(*operands):
    vmem = pl.BlockSpec(memory_space=pltpu.VMEM)
    return pl.pallas_call(
        place_kernel,
        out_shape=jax.ShapeDtypeStruct((2 * N_LAYER, BS, WIDTH // N_LAYER), jnp.bfloat16),
        in_specs=[vmem] * len(operands),
        out_specs=vmem,
        scratch_shapes=[
            pltpu.VMEM((2 * BS, N_YH * WINDOW), jnp.bfloat16),
            pltpu.VMEM((2 * BS, WIDTH), jnp.float32),
            pltpu.VMEM((16, 128), jnp.int32),
            pltpu.SMEM((16, 128), jnp.int32),
            pltpu.SemaphoreType.DMA,
        ]
        + [pltpu.VMEM((DEPTH, WIDTH), jnp.bfloat16)] * GROUP
        + [pltpu.VMEM((BODY, 128), jnp.bfloat16)] * GROUP,
        compiler_params=pltpu.CompilerParams(vmem_limit_bytes=24 * 1024 * 1024),
        cost_estimate=pl.CostEstimate(
            flops=2 * 128 * 3072 * 2048, bytes_accessed=4 << 20, transcendentals=0
        ),
    )(*operands)


def nothing_kernel(whole, when, out):
    pass


def after(whole, when):
    return pl.pallas_call(
        nothing_kernel,
        out_shape=jax.ShapeDtypeStruct(whole.shape, whole.dtype),
        in_specs=[pl.BlockSpec(memory_space=pl.ANY)] * 2,
        out_specs=pl.BlockSpec(memory_space=pl.ANY),
        input_output_aliases={0: 0},
    )(whole, when)


def shards(left_blocks, left_coords, right_blocks, right_coords):
    mine, piece = pack(
        right_blocks.reshape(SLOTS, BS, BS),
        right_coords.reshape(SLOTS, 2).T,
        left_blocks.reshape(2, BS, BS),
        left_coords.reshape(2, 2),
    )
    yl = lax.axis_index("yl")
    own = lax.all_to_all(mine, "yh", 0, 0)
    pieces = lax.all_gather(piece, "col")
    wanted = lax.dynamic_slice_in_dim(pieces.reshape(N_YH, 3, LMSG, 128), 1 - yl, 2, 1)
    wanted = wanted.reshape(2 * N_YH, LMSG, 128)
    other = lax.ppermute(after(own, pieces), "core", [(0, 1), (1, 0)])
    pieces_other = lax.ppermute(wanted, "yl", [(0, 1), (1, 0)])
    part = multiply(own, other, pieces, pieces_other)
    parts = lax.all_to_all(part, ("yl", "layer"), 0, 0)
    total = jnp.sum(parts.astype(jnp.float32), axis=0)
    return total.reshape(1, BS, COLUMNS // N_LAYER, BS)


def solution(mesh):
    grid = Mesh(mesh.devices.reshape(N_YH, 2, 2, N_COL, N_LAYER), ("yh", "yl", "core", "col", "layer"))
    row = ("yh", "yl", "core")
    return jax.shard_map(
        shards,
        mesh=grid,
        in_specs=(
            P(row, "col", "layer", None, None, None),
            P(row, "col", "layer", None, None),
            P(row, "col", "layer", None, None, None),
            P(row, "col", "layer", None, None),
        ),
        out_specs=P(row, None, ("col", "layer"), None),
        check_vma=False,
    )
```

```python
import jax
import jax.numpy as jnp
from jax import lax
from jax.experimental import pallas as pl
from jax.experimental.pallas import tpu as pltpu
from jax.sharding import Mesh
from jax.sharding import PartitionSpec as P

NB = 384
BS = 64
N_YH = 4
N_COL = 12
N_LAYER = 4
SLOTS = 32
PAIRS = SLOTS // 2
BODY = PAIRS * BS
MSG = BODY + 16
LMSG = BS + 16
INNER = 6
COLUMNS = NB // N_COL
PIECE = NB // N_LAYER // N_COL
DEPTH = INNER * BS
WIDTH = COLUMNS * BS
GROUP = 4
WINDOW = 2 * PIECE * BS


def pack_kernel(right, right_where, left, left_where, out, piece, tail):
    y = lax.axis_index("yh") * 2 + lax.axis_index("yl")
    core = lax.axis_index("core")
    col = lax.axis_index("col")
    base = lax.axis_index("layer") * (NB // N_LAYER)
    for p in range(PAIRS):
        out[p * BS : (p + 1) * BS, :] = jnp.concatenate([right[p], right[p + PAIRS]], axis=-1)
    tail[...] = jnp.zeros_like(tail)
    inner = right_where[0:1, :] - (base + (y * 2 + core) * INNER)
    column = right_where[1:2, :] - col * COLUMNS
    tail[0:1, 0:SLOTS] = inner.astype(jnp.float32)
    tail[1:2, 0:SLOTS] = column.astype(jnp.float32)
    out[BODY:MSG, :] = tail[...].astype(jnp.bfloat16)
    lane = lax.broadcasted_iota(jnp.int32, (16, 128), 1)
    first = jnp.broadcast_to(left_where[0:1, 1:2], (16, 128))
    second = jnp.broadcast_to(left_where[1:2, 1:2], (16, 128))
    at = jnp.where(lane < BS, first, second) - (base + col * PIECE)
    at = at.astype(jnp.float32).astype(jnp.bfloat16)
    pair = jnp.concatenate([left[0], left[1]], axis=-1)
    piece[:BS, :] = pair
    piece[BS:, :] = at


def pack(right, right_where, left, left_where):
    vmem = pl.BlockSpec(memory_space=pltpu.VMEM)
    return pl.pallas_call(
        pack_kernel,
        out_shape=(
            jax.ShapeDtypeStruct((MSG, 128), jnp.bfloat16),
            jax.ShapeDtypeStruct((LMSG, 128), jnp.bfloat16),
        ),
        in_specs=[vmem] * 4,
        out_specs=(vmem, vmem),
        scratch_shapes=[pltpu.VMEM((16, 128), jnp.float32)],
        cost_estimate=pl.CostEstimate(flops=0, bytes_accessed=2 << 20, transcendentals=0),
    )(right, right_where, left, left_where)


def half_swap():
    to = lax.broadcasted_iota(jnp.int32, (128, 128), 1)
    frm = lax.broadcasted_iota(jnp.int32, (128, 128), 0)
    return (to == (frm + BS) % 128).astype(jnp.bfloat16)


def read_places(blocks, where, places, sem):
    for i, block in enumerate(blocks):
        tail = block[BODY:MSG, :].astype(jnp.float32).astype(jnp.int32)
        where[2 * i : 2 * i + 2, :] = tail[0:2, :]
    copy = pltpu.make_async_copy(where, places, sem)
    copy.start()
    return copy


def place_slots(blocks, first, panels, swapped, places):
    lane = lax.broadcasted_iota(jnp.int32, (BS, 128), 1)
    low = (lane < BS).astype(jnp.bfloat16)
    high = (lane >= BS).astype(jnp.bfloat16)

    def place(p, carry):
        at = pl.ds(pl.multiple_of(p * BS, BS), BS)
        for half in range(2):
            for i, block in enumerate(blocks):
                k = places[2 * (first + i), p + half * PAIRS]
                n = places[2 * (first + i) + 1, p + half * PAIRS]
                odd = n & 1
                value = jnp.where(odd == half, block[at, :], swapped[i][at, :])
                value = value * jnp.where(odd == 1, high, low)
                rows = pl.ds(pl.multiple_of(k * BS, BS), BS)
                lanes = pl.ds(pl.multiple_of((n >> 1) * 128, 128), 128)
                panels[i][rows, lanes] = panels[i][rows, lanes] + value
        return carry

    lax.fori_loop(0, PAIRS, place, 0, unroll=2)


def place_kernel(gathered, left_own, left_other, out, left, total, where, places, sem, *scratch):
    panels, swapped = scratch[:GROUP], scratch[GROUP:]
    yl = lax.axis_index("yl")
    blocks = [gathered.at[j] for j in range(2 * N_YH)]
    copy = read_places(blocks, where, places, sem)
    swap = half_swap()

    lane = lax.broadcasted_iota(jnp.int32, (BS, 128), 1)
    upper = (lane >= BS).astype(jnp.float32)
    for src, at in ((left_own, yl), (left_other, 1 - yl)):
        rows = pl.ds(pl.multiple_of(at * BS, BS), BS)
        for q in range(N_YH):
            for u in range(2):
                whole = src[3 * q + yl + u] if src is left_own else src[2 * q + u]
                there = jnp.dot(whole, swap, preferred_element_type=jnp.float32)
                here = whole.astype(jnp.float32)
                for g in range(PIECE // 2):
                    want = upper + 2.0 * g
                    value = jnp.where(here[BS : BS + 1] == want, here[:BS], 0.0)
                    value = value + jnp.where(there[BS : BS + 1] == want, there[:BS], 0.0)
                    at_lane = q * WINDOW + (u * PIECE + 2 * g) * BS
                    left[rows, at_lane : at_lane + 128] = value.astype(jnp.bfloat16)

    for j0 in range(0, 2 * N_YH, GROUP):
        now = blocks[j0 : j0 + GROUP]
        for i, block in enumerate(now):
            panels[i][...] = jnp.zeros_like(panels[i])
            swapped[i][...] = jnp.dot(
                block[:BODY, :], swap, preferred_element_type=jnp.float32
            ).astype(jnp.bfloat16)
        if j0 == 0:
            copy.wait()
        place_slots(now, j0, panels, swapped, places)
        for i in range(len(now)):
            j = j0 + i
            start = (j // 2) * WINDOW + yl * (4 * BS) + (j % 2) * DEPTH
            at = pl.ds(pl.multiple_of(start, 128), DEPTH)
            part = jnp.dot(left[:, at], panels[i][...], preferred_element_type=jnp.float32)
            total[...] = part if j == 0 else total[...] + part
    share = WIDTH // N_LAYER
    for m in range(2):
        for s in range(N_LAYER):
            out[m * N_LAYER + s] = total[m * BS : (m + 1) * BS, s * share : (s + 1) * share].astype(
                jnp.bfloat16
            )


def multiply(*operands):
    vmem = pl.BlockSpec(memory_space=pltpu.VMEM)
    return pl.pallas_call(
        place_kernel,
        out_shape=jax.ShapeDtypeStruct((2 * N_LAYER, BS, WIDTH // N_LAYER), jnp.bfloat16),
        in_specs=[vmem] * len(operands),
        out_specs=vmem,
        scratch_shapes=[
            pltpu.VMEM((2 * BS, N_YH * WINDOW), jnp.bfloat16),
            pltpu.VMEM((2 * BS, WIDTH), jnp.float32),
            pltpu.VMEM((16, 128), jnp.int32),
            pltpu.SMEM((16, 128), jnp.int32),
            pltpu.SemaphoreType.DMA,
        ]
        + [pltpu.VMEM((DEPTH, WIDTH), jnp.bfloat16)] * GROUP
        + [pltpu.VMEM((BODY, 128), jnp.bfloat16)] * GROUP,
        compiler_params=pltpu.CompilerParams(vmem_limit_bytes=24 * 1024 * 1024),
        cost_estimate=pl.CostEstimate(
            flops=2 * 128 * 3072 * 2048, bytes_accessed=4 << 20, transcendentals=0
        ),
    )(*operands)


def shards(left_blocks, left_coords, right_blocks, right_coords):
    mine, piece = pack(
        right_blocks.reshape(SLOTS, BS, BS),
        right_coords.reshape(SLOTS, 2).T,
        left_blocks.reshape(2, BS, BS),
        left_coords.reshape(2, 2),
    )
    yl = lax.axis_index("yl")
    gathered = lax.all_gather(mine, ("yh", "core"))
    pieces = lax.all_gather(piece, "col")
    wanted = lax.dynamic_slice_in_dim(pieces.reshape(N_YH, 3, LMSG, 128), 1 - yl, 2, 1)
    wanted = wanted.reshape(2 * N_YH, LMSG, 128)
    pieces_other = lax.ppermute(wanted, "yl", [(0, 1), (1, 0)])
    part = multiply(gathered, pieces, pieces_other)
    parts = lax.all_to_all(part, ("yl", "layer"), 0, 0)
    total = jnp.sum(parts.astype(jnp.float32), axis=0)
    return total.reshape(1, BS, COLUMNS // N_LAYER, BS)


def solution(mesh):
    grid = Mesh(mesh.devices.reshape(N_YH, 2, 2, N_COL, N_LAYER), ("yh", "yl", "core", "col", "layer"))
    row = ("yh", "yl", "core")
    return jax.shard_map(
        shards,
        mesh=grid,
        in_specs=(
            P(row, "col", "layer", None, None, None),
            P(row, "col", "layer", None, None),
            P(row, "col", "layer", None, None, None),
            P(row, "col", "layer", None, None),
        ),
        out_specs=P(row, None, ("col", "layer"), None),
        check_vma=False,
    )
```

```python
import jax
import jax.numpy as jnp
from jax import lax
from jax.experimental import pallas as pl
from jax.experimental.pallas import tpu as pltpu
from jax.sharding import Mesh
from jax.sharding import PartitionSpec as P

NB = 384
BS = 64
N_YH = 4
N_COL = 12
N_LAYER = 4
SLOTS = 32
PAIRS = SLOTS // 2
BODY = PAIRS * BS
MSG = BODY + 16
LMSG = BS + 16
INNER = 6
COLUMNS = NB // N_COL
PIECE = NB // N_LAYER // N_COL
DEPTH = INNER * BS
WIDTH = COLUMNS * BS
NEAR = 3
CUT = 512
WINDOW = 2 * PIECE * BS


def pack_kernel(right, right_where, left, left_where, out, piece, tail):
    y = lax.axis_index("yh") * 2 + lax.axis_index("yl")
    core = lax.axis_index("core")
    col = lax.axis_index("col")
    base = lax.axis_index("layer") * (NB // N_LAYER)
    for p in range(PAIRS):
        out[p * BS : (p + 1) * BS, :] = jnp.concatenate([right[p], right[p + PAIRS]], axis=-1)
    tail[...] = jnp.zeros_like(tail)
    inner = right_where[0:1, :] - (base + (y * 2 + core) * INNER)
    column = right_where[1:2, :] - col * COLUMNS
    tail[0:1, 0:SLOTS] = inner.astype(jnp.float32)
    tail[1:2, 0:SLOTS] = column.astype(jnp.float32)
    out[BODY:MSG, :] = tail[...].astype(jnp.bfloat16)
    lane = lax.broadcasted_iota(jnp.int32, (16, 128), 1)
    first = jnp.broadcast_to(left_where[0:1, 1:2], (16, 128))
    second = jnp.broadcast_to(left_where[1:2, 1:2], (16, 128))
    at = jnp.where(lane < BS, first, second) - (base + col * PIECE)
    at = at.astype(jnp.float32).astype(jnp.bfloat16)
    pair = jnp.concatenate([left[0], left[1]], axis=-1)
    piece[:BS, :] = pair
    piece[BS:, :] = at


def pack(right, right_where, left, left_where):
    vmem = pl.BlockSpec(memory_space=pltpu.VMEM)
    return pl.pallas_call(
        pack_kernel,
        out_shape=(
            jax.ShapeDtypeStruct((MSG, 128), jnp.bfloat16),
            jax.ShapeDtypeStruct((LMSG, 128), jnp.bfloat16),
        ),
        in_specs=[vmem] * 4,
        out_specs=(vmem, vmem),
        scratch_shapes=[pltpu.VMEM((16, 128), jnp.float32)],
        cost_estimate=pl.CostEstimate(flops=0, bytes_accessed=2 << 20, transcendentals=0),
    )(right, right_where, left, left_where)


def half_swap():
    to = lax.broadcasted_iota(jnp.int32, (128, 128), 1)
    frm = lax.broadcasted_iota(jnp.int32, (128, 128), 0)
    return (to == (frm + BS) % 128).astype(jnp.bfloat16)


def place_slots(blocks, panels, swapped, places):
    lane = lax.broadcasted_iota(jnp.int32, (BS, 128), 1)
    low = (lane < BS).astype(jnp.bfloat16)
    high = (lane >= BS).astype(jnp.bfloat16)

    def place(p, carry):
        at = pl.ds(pl.multiple_of(p * BS, BS), BS)
        for half in range(2):
            for i, block in enumerate(blocks):
                k = places[2 * i, p + half * PAIRS]
                n = places[2 * i + 1, p + half * PAIRS]
                odd = n & 1
                value = jnp.where(odd == half, block[at, :], swapped[i][at, :])
                value = value * jnp.where(odd == 1, high, low)
                rows = pl.ds(pl.multiple_of(k * BS, BS), BS)
                lanes = pl.ds(pl.multiple_of((n >> 1) * 128, 128), 128)
                panels[i][rows, lanes] = panels[i][rows, lanes] + value
        return carry

    lax.fori_loop(0, PAIRS, place, 0, unroll=2)


def read_places(blocks, where, places, sem):
    for i, block in enumerate(blocks):
        tail = block[BODY:MSG, :].astype(jnp.float32).astype(jnp.int32)
        where[2 * i : 2 * i + 2, :] = tail[0:2, :]
    copy = pltpu.make_async_copy(where, places, sem)
    copy.start()
    return copy


def fill_panels(blocks, panels, swapped, places, copy):
    swap = half_swap()
    for i, block in enumerate(blocks):
        panels[i][...] = jnp.zeros_like(panels[i])
        swapped[i][...] = jnp.dot(
            block[:BODY, :], swap, preferred_element_type=jnp.float32
        ).astype(jnp.bfloat16)
    copy.wait()
    place_slots(blocks, panels, swapped, places)


def scratch_for(blocks):
    return (
        [
            pltpu.VMEM((16, 128), jnp.int32),
            pltpu.SMEM((16, 128), jnp.int32),
            pltpu.SemaphoreType.DMA,
            pltpu.SemaphoreType.DMA((NEAR,)),
        ]
        + [pltpu.VMEM((DEPTH, WIDTH), jnp.bfloat16)] * blocks
        + [pltpu.VMEM((BODY, 128), jnp.bfloat16)] * blocks
    )


def early_kernel(near, out, where, places, sem, sems, *scratch):
    panels, swapped = scratch[:NEAR], scratch[NEAR:]
    blocks = [near.at[j] for j in range(NEAR)]
    fill_panels(blocks, panels, swapped, places, read_places(blocks, where, places, sem))
    copies = [pltpu.make_async_copy(panels[j], out.at[j], sems.at[j]) for j in range(NEAR)]
    for copy in copies:
        copy.start()
    for copy in copies:
        copy.wait()


def early(near):
    return pl.pallas_call(
        early_kernel,
        out_shape=pltpu.HBM((NEAR, DEPTH, WIDTH), jnp.bfloat16),
        in_specs=[pl.BlockSpec(memory_space=pltpu.VMEM)],
        out_specs=pl.BlockSpec(memory_space=pltpu.HBM),
        scratch_shapes=scratch_for(NEAR),
        compiler_params=pltpu.CompilerParams(vmem_limit_bytes=12 * 1024 * 1024),
        cost_estimate=pl.CostEstimate(flops=0, bytes_accessed=10 << 20, transcendentals=0),
    )(near)


def multiply_kernel(pieces, ready, far, near_other, far_other, out, *scratch):
    (left, total, *held), (where, places, sem, sems) = scratch[: 2 + NEAR], scratch[2 + NEAR : 6 + NEAR]
    panels, swapped = scratch[6 + NEAR : 11 + NEAR], scratch[11 + NEAR :]
    blocks = [far] + [near_other.at[j] for j in range(NEAR)] + [far_other]
    copies = [pltpu.make_async_copy(ready.at[j], held[j], sems.at[j]) for j in range(NEAR)]
    for copy in copies:
        copy.start()
    copy = read_places(blocks, where, places, sem)
    yl = lax.axis_index("yl")
    core = lax.axis_index("core")
    yh = lax.axis_index("yh")
    swap = half_swap()

    lane = lax.broadcasted_iota(jnp.int32, (BS, 128), 1)
    upper = (lane >= BS).astype(jnp.float32)
    for m, at in ((0, yl), (1, 1 - yl)):
        rows = pl.ds(pl.multiple_of(at * BS, BS), BS)
        for q in range(N_YH):
            for u in range(2):
                piece = pieces.at[3 * q + yl + u]
                here = piece[m * BS : (m + 1) * BS, :]
                marks = piece[2 * BS :, :]
                there = jnp.dot(here, swap, preferred_element_type=jnp.float32)
                k_there = jnp.dot(marks, swap, preferred_element_type=jnp.float32)[m : m + 1]
                here = here.astype(jnp.float32)
                k_here = marks.astype(jnp.float32)[m : m + 1]
                for g in range(PIECE // 2):
                    want = upper + 2.0 * g
                    value = jnp.where(k_here == want, here, 0.0)
                    value = value + jnp.where(k_there == want, there, 0.0)
                    at_lane = q * WINDOW + (u * PIECE + 2 * g) * BS
                    left[rows, at_lane : at_lane + 128] = value.astype(jnp.bfloat16)

    fill_panels(blocks, panels, swapped, places, copy)
    for copy in copies:
        copy.wait()
    order = ((0, core), (3, core), (1, core), (2, core))
    order += tuple((away, 1 - core) for away, _ in order)
    for j, (away, side) in enumerate(order):
        panel = held[j] if j < NEAR else panels[j - NEAR]
        start = ((yh + away) % N_YH) * WINDOW + yl * (4 * BS) + side * DEPTH
        at = pl.ds(pl.multiple_of(start, 128), DEPTH)
        part = jnp.dot(left[:, at], panel[...], preferred_element_type=jnp.float32)
        total[...] = part if j == 0 else total[...] + part
    share = WIDTH // N_LAYER
    for m in range(2):
        for s in range(N_LAYER):
            out[m * N_LAYER + s] = total[m * BS : (m + 1) * BS, s * share : (s + 1) * share].astype(
                jnp.bfloat16
            )


def multiply(pieces, ready, far, near_other, far_other):
    vmem = pl.BlockSpec(memory_space=pltpu.VMEM)
    return pl.pallas_call(
        multiply_kernel,
        out_shape=jax.ShapeDtypeStruct((2 * N_LAYER, BS, WIDTH // N_LAYER), jnp.bfloat16),
        in_specs=[vmem, pl.BlockSpec(memory_space=pltpu.HBM), vmem, vmem, vmem],
        out_specs=vmem,
        scratch_shapes=[
            pltpu.VMEM((2 * BS, N_YH * WINDOW), jnp.bfloat16),
            pltpu.VMEM((2 * BS, WIDTH), jnp.float32),
        ]
        + [pltpu.VMEM((DEPTH, WIDTH), jnp.bfloat16)] * NEAR
        + scratch_for(5),
        compiler_params=pltpu.CompilerParams(vmem_limit_bytes=24 * 1024 * 1024),
        cost_estimate=pl.CostEstimate(
            flops=2 * 128 * 3072 * 2048, bytes_accessed=4 << 20, transcendentals=0
        ),
    )(pieces, pltpu.with_memory_space_constraint(ready, pltpu.HBM), far, near_other, far_other)


def spread_kernel(mine, theirs, out):
    first = lax.broadcasted_iota(jnp.int32, (16, 128), 0) == 0
    tail = jnp.where(first, mine[BS:, :].astype(jnp.float32), theirs[BS:, :].astype(jnp.float32))
    for c in range(N_COL):
        out[c, :BS, :] = mine[:BS, :]
        out[c, BS : 2 * BS, :] = theirs[:BS, :]
        out[c, 2 * BS :, :] = tail.astype(jnp.bfloat16)


def spread(mine, theirs):
    vmem = pl.BlockSpec(memory_space=pltpu.VMEM)
    return pl.pallas_call(
        spread_kernel,
        out_shape=jax.ShapeDtypeStruct((N_COL, 2 * BS + 16, 128), jnp.bfloat16),
        in_specs=[vmem] * 2,
        out_specs=vmem,
        cost_estimate=pl.CostEstimate(flops=0, bytes_accessed=1 << 20, transcendentals=0),
    )(mine, theirs)


def shards(left_blocks, left_coords, right_blocks, right_coords):
    mine, piece = pack(
        right_blocks.reshape(SLOTS, BS, BS),
        right_coords.reshape(SLOTS, 2).T,
        left_blocks.reshape(2, BS, BS),
        left_coords.reshape(2, 2),
    )
    up = [(i, (i + 1) % N_YH) for i in range(N_YH)]
    down = [(i, (i - 1) % N_YH) for i in range(N_YH)]
    cross = [(0, 1), (1, 0)]
    neighbour = lax.ppermute(piece, "yl", cross)
    below = lax.ppermute(mine, "yh", up)
    above = lax.ppermute(mine, "yh", down)
    pieces = lax.all_to_all(spread(piece, neighbour), "col", 0, 0)
    far_low = lax.ppermute(below[:CUT], "yh", up)
    far_high = lax.ppermute(above[CUT:], "yh", down)
    near = jnp.stack([mine, below, above])
    near_other = lax.ppermute(near, "core", cross)
    far = jnp.concatenate([far_low, far_high])
    far_other = lax.ppermute(far, "core", cross)
    part = multiply(pieces, early(near), far, near_other, far_other)
    parts = lax.all_to_all(part, ("yl", "layer"), 0, 0)
    total = jnp.sum(parts.astype(jnp.float32), axis=0)
    return total.reshape(1, BS, COLUMNS // N_LAYER, BS)


def solution(mesh):
    grid = Mesh(mesh.devices.reshape(N_YH, 2, 2, N_COL, N_LAYER), ("yh", "yl", "core", "col", "layer"))
    row = ("yh", "yl", "core")
    return jax.shard_map(
        shards,
        mesh=grid,
        in_specs=(
            P(row, "col", "layer", None, None, None),
            P(row, "col", "layer", None, None),
            P(row, "col", "layer", None, None, None),
            P(row, "col", "layer", None, None),
        ),
        out_specs=P(row, None, ("col", "layer"), None),
        check_vma=False,
    )
```

```python
import jax
import jax.numpy as jnp
from jax import lax
from jax.experimental import pallas as pl
from jax.experimental.pallas import tpu as pltpu
from jax.sharding import Mesh
from jax.sharding import PartitionSpec as P

NB = 384
BS = 64
N_YH = 4
N_COL = 12
N_LAYER = 4
SLOTS = 32
PAIRS = SLOTS // 2
BODY = PAIRS * BS
MSG = BODY + 16
LMSG = BS + 16
INNER = 6
COLUMNS = NB // N_COL
PIECE = NB // N_LAYER // N_COL
DEPTH = INNER * BS
WIDTH = COLUMNS * BS
NEAR = 4
WINDOW = 2 * PIECE * BS


def pack_kernel(right, right_where, left, left_where, out, piece, tail):
    y = lax.axis_index("yh") * 2 + lax.axis_index("yl")
    core = lax.axis_index("core")
    col = lax.axis_index("col")
    base = lax.axis_index("layer") * (NB // N_LAYER)
    for p in range(PAIRS):
        out[p * BS : (p + 1) * BS, :] = jnp.concatenate([right[p], right[p + PAIRS]], axis=-1)
    tail[...] = jnp.zeros_like(tail)
    inner = right_where[0:1, :] - (base + (y * 2 + core) * INNER)
    column = right_where[1:2, :] - col * COLUMNS
    tail[0:1, 0:SLOTS] = inner.astype(jnp.float32)
    tail[1:2, 0:SLOTS] = column.astype(jnp.float32)
    out[BODY:MSG, :] = tail[...].astype(jnp.bfloat16)
    lane = lax.broadcasted_iota(jnp.int32, (16, 128), 1)
    first = jnp.broadcast_to(left_where[0:1, 1:2], (16, 128))
    second = jnp.broadcast_to(left_where[1:2, 1:2], (16, 128))
    at = jnp.where(lane < BS, first, second) - (base + col * PIECE)
    at = at.astype(jnp.float32).astype(jnp.bfloat16)
    pair = jnp.concatenate([left[0], left[1]], axis=-1)
    piece[:BS, :] = pair
    piece[BS:, :] = at


def pack(right, right_where, left, left_where):
    vmem = pl.BlockSpec(memory_space=pltpu.VMEM)
    return pl.pallas_call(
        pack_kernel,
        out_shape=(
            jax.ShapeDtypeStruct((MSG, 128), jnp.bfloat16),
            jax.ShapeDtypeStruct((LMSG, 128), jnp.bfloat16),
        ),
        in_specs=[vmem] * 4,
        out_specs=(vmem, vmem),
        scratch_shapes=[pltpu.VMEM((16, 128), jnp.float32)],
        cost_estimate=pl.CostEstimate(flops=0, bytes_accessed=2 << 20, transcendentals=0),
    )(right, right_where, left, left_where)


def half_swap():
    to = lax.broadcasted_iota(jnp.int32, (128, 128), 1)
    frm = lax.broadcasted_iota(jnp.int32, (128, 128), 0)
    return (to == (frm + BS) % 128).astype(jnp.bfloat16)


def place_slots(blocks, panels, swapped, places):
    lane = lax.broadcasted_iota(jnp.int32, (BS, 128), 1)
    low = (lane < BS).astype(jnp.bfloat16)
    high = (lane >= BS).astype(jnp.bfloat16)

    def place(p, carry):
        at = pl.ds(pl.multiple_of(p * BS, BS), BS)
        for half in range(2):
            for i, block in enumerate(blocks):
                k = places[2 * i, p + half * PAIRS]
                n = places[2 * i + 1, p + half * PAIRS]
                odd = n & 1
                value = jnp.where(odd == half, block[at, :], swapped[i][at, :])
                value = value * jnp.where(odd == 1, high, low)
                rows = pl.ds(pl.multiple_of(k * BS, BS), BS)
                lanes = pl.ds(pl.multiple_of((n >> 1) * 128, 128), 128)
                panels[i][rows, lanes] = panels[i][rows, lanes] + value
        return carry

    lax.fori_loop(0, PAIRS, place, 0, unroll=2)


def read_places(blocks, where, places, sem):
    for i, block in enumerate(blocks):
        tail = block[BODY:MSG, :].astype(jnp.float32).astype(jnp.int32)
        where[2 * i : 2 * i + 2, :] = tail[0:2, :]
    copy = pltpu.make_async_copy(where, places, sem)
    copy.start()
    return copy


def fill_panels(blocks, panels, swapped, places, copy):
    swap = half_swap()
    for i, block in enumerate(blocks):
        panels[i][...] = jnp.zeros_like(panels[i])
        swapped[i][...] = jnp.dot(
            block[:BODY, :], swap, preferred_element_type=jnp.float32
        ).astype(jnp.bfloat16)
    copy.wait()
    place_slots(blocks, panels, swapped, places)


def scratch_for(blocks):
    return (
        [
            pltpu.VMEM((16, 128), jnp.int32),
            pltpu.SMEM((16, 128), jnp.int32),
            pltpu.SemaphoreType.DMA,
            pltpu.SemaphoreType.DMA((NEAR,)),
        ]
        + [pltpu.VMEM((DEPTH, WIDTH), jnp.bfloat16)] * blocks
        + [pltpu.VMEM((BODY, 128), jnp.bfloat16)] * blocks
    )


def early_kernel(first, second, out, where, places, sem, sems, *scratch):
    panels, swapped = scratch[:NEAR], scratch[NEAR:]
    blocks = [first.at[0], first.at[1], second.at[0], second.at[1]]
    fill_panels(blocks, panels, swapped, places, read_places(blocks, where, places, sem))
    copies = [pltpu.make_async_copy(panels[j], out.at[j], sems.at[j]) for j in range(NEAR)]
    for copy in copies:
        copy.start()
    for copy in copies:
        copy.wait()


def early(first, second):
    return pl.pallas_call(
        early_kernel,
        out_shape=pltpu.HBM((NEAR, DEPTH, WIDTH), jnp.bfloat16),
        in_specs=[pl.BlockSpec(memory_space=pltpu.VMEM)] * 2,
        out_specs=pl.BlockSpec(memory_space=pltpu.HBM),
        scratch_shapes=scratch_for(NEAR),
        compiler_params=pltpu.CompilerParams(vmem_limit_bytes=14 * 1024 * 1024),
        cost_estimate=pl.CostEstimate(flops=40_000_000_000, bytes_accessed=10 << 20, transcendentals=0),
    )(first, second)


def multiply_kernel(left_own, left_other, ready, first, second, out, *scratch):
    (left, total, *held), (where, places, sem, sems) = scratch[: 2 + NEAR], scratch[2 + NEAR : 6 + NEAR]
    panels, swapped = scratch[6 + NEAR : 6 + 2 * NEAR], scratch[6 + 2 * NEAR :]
    blocks = [first.at[0], first.at[1], second.at[0], second.at[1]]
    copies = [pltpu.make_async_copy(ready.at[j], held[j], sems.at[j]) for j in range(NEAR)]
    for copy in copies:
        copy.start()
    copy = read_places(blocks, where, places, sem)
    yl = lax.axis_index("yl")
    core = lax.axis_index("core")
    yh = lax.axis_index("yh")
    swap = half_swap()

    lane = lax.broadcasted_iota(jnp.int32, (BS, 128), 1)
    upper = (lane >= BS).astype(jnp.float32)
    for src, at in ((left_own, yl), (left_other, 1 - yl)):
        rows = pl.ds(pl.multiple_of(at * BS, BS), BS)
        for q in range(N_YH):
            for u in range(2):
                whole = src[3 * q + yl + u] if src is left_own else src[2 * q + u]
                there = jnp.dot(whole, swap, preferred_element_type=jnp.float32)
                here = whole.astype(jnp.float32)
                for g in range(PIECE // 2):
                    want = upper + 2.0 * g
                    value = jnp.where(here[BS : BS + 1] == want, here[:BS], 0.0)
                    value = value + jnp.where(there[BS : BS + 1] == want, there[:BS], 0.0)
                    at_lane = q * WINDOW + (u * PIECE + 2 * g) * BS
                    left[rows, at_lane : at_lane + 128] = value.astype(jnp.bfloat16)

    fill_panels(blocks, panels, swapped, places, copy)
    for copy in copies:
        copy.wait()
    order = tuple((away, core) for away in (0, 3, 1, 2))
    order += tuple((away, 1 - core) for away, _ in order)
    for j, (away, side) in enumerate(order):
        panel = held[j] if j < NEAR else panels[j - NEAR]
        start = ((yh + away) % N_YH) * WINDOW + yl * (4 * BS) + side * DEPTH
        at = pl.ds(pl.multiple_of(start, 128), DEPTH)
        part = jnp.dot(left[:, at], panel[...], preferred_element_type=jnp.float32)
        total[...] = part if j == 0 else total[...] + part
    share = WIDTH // N_LAYER
    for m in range(2):
        for s in range(N_LAYER):
            out[m * N_LAYER + s] = total[m * BS : (m + 1) * BS, s * share : (s + 1) * share].astype(
                jnp.bfloat16
            )


def multiply(left_own, left_other, ready, first, second):
    vmem = pl.BlockSpec(memory_space=pltpu.VMEM)
    return pl.pallas_call(
        multiply_kernel,
        out_shape=jax.ShapeDtypeStruct((2 * N_LAYER, BS, WIDTH // N_LAYER), jnp.bfloat16),
        in_specs=[vmem, vmem, pl.BlockSpec(memory_space=pltpu.HBM), vmem, vmem],
        out_specs=vmem,
        scratch_shapes=[
            pltpu.VMEM((2 * BS, N_YH * WINDOW), jnp.bfloat16),
            pltpu.VMEM((2 * BS, WIDTH), jnp.float32),
        ]
        + [pltpu.VMEM((DEPTH, WIDTH), jnp.bfloat16)] * NEAR
        + scratch_for(NEAR),
        compiler_params=pltpu.CompilerParams(vmem_limit_bytes=24 * 1024 * 1024),
        cost_estimate=pl.CostEstimate(
            flops=2 * 128 * 3072 * 2048, bytes_accessed=4 << 20, transcendentals=0
        ),
    )(left_own, left_other, pltpu.with_memory_space_constraint(ready, pltpu.HBM), first, second)


def spread_kernel(piece, when, out):
    del when
    for c in range(N_COL):
        out[c] = piece[...]


def spread(piece, when):
    vmem = pl.BlockSpec(memory_space=pltpu.VMEM)
    return pl.pallas_call(
        spread_kernel,
        out_shape=jax.ShapeDtypeStruct((N_COL, LMSG, 128), jnp.bfloat16),
        in_specs=[vmem, pl.BlockSpec(memory_space=pl.ANY)],
        out_specs=vmem,
        cost_estimate=pl.CostEstimate(flops=0, bytes_accessed=1 << 20, transcendentals=0),
    )(piece, when)


def shards(left_blocks, left_coords, right_blocks, right_coords):
    mine, piece = pack(
        right_blocks.reshape(SLOTS, BS, BS),
        right_coords.reshape(SLOTS, 2).T,
        left_blocks.reshape(2, BS, BS),
        left_coords.reshape(2, 2),
    )
    yl = lax.axis_index("yl")
    away = [[(i, (i + d) % N_YH) for i in range(N_YH)] for d in range(N_YH)]
    cross = [(0, 1), (1, 0)]
    below, far, above = (lax.ppermute(mine, "yh", away[d]) for d in (1, 2, 3))
    tick = lax.ppermute(piece[BS:], "core", cross)
    pieces = lax.all_to_all(spread(piece, tick), "col", 0, 0)
    wanted = lax.dynamic_slice_in_dim(pieces.reshape(N_YH, 3, LMSG, 128), 1 - yl, 2, 1)
    pieces_other = lax.ppermute(wanted.reshape(2 * N_YH, LMSG, 128), "yl", cross)
    near = (jnp.stack([mine, below]), jnp.stack([above, far]))
    near_other = [lax.ppermute(two, "core", cross) for two in near]
    part = multiply(pieces, pieces_other, early(*near), *near_other)
    parts = lax.all_to_all(part, ("yl", "layer"), 0, 0)
    total = jnp.sum(parts.astype(jnp.float32), axis=0)
    return total.reshape(1, BS, COLUMNS // N_LAYER, BS)


def solution(mesh):
    grid = Mesh(mesh.devices.reshape(N_YH, 2, 2, N_COL, N_LAYER), ("yh", "yl", "core", "col", "layer"))
    row = ("yh", "yl", "core")
    return jax.shard_map(
        shards,
        mesh=grid,
        in_specs=(
            P(row, "col", "layer", None, None, None),
            P(row, "col", "layer", None, None),
            P(row, "col", "layer", None, None, None),
            P(row, "col", "layer", None, None),
        ),
        out_specs=P(row, None, ("col", "layer"), None),
        check_vma=False,
    )
```

```python
import jax
import jax.numpy as jnp
from jax import lax
from jax.experimental import pallas as pl
from jax.experimental.pallas import tpu as pltpu
from jax.sharding import Mesh
from jax.sharding import PartitionSpec as P

NB = 384
BS = 64
N_YH = 4
N_COL = 12
N_LAYER = 4
SLOTS = 32
PAIRS = SLOTS // 2
BODY = PAIRS * BS
MSG = BODY + 16
LMSG = BS + 16
INNER = 6
COLUMNS = NB // N_COL
PIECE = NB // N_LAYER // N_COL
DEPTH = INNER * BS
WIDTH = COLUMNS * BS
GROUP = 4
WINDOW = 2 * PIECE * BS


def pack_left_kernel(left, left_where, out):
    base = lax.axis_index("layer") * (NB // N_LAYER) + lax.axis_index("col") * PIECE
    out[:BS, :] = jnp.concatenate([left[0], left[1]], axis=-1)
    lane = lax.broadcasted_iota(jnp.int32, (16, 128), 1)
    first = jnp.broadcast_to(left_where[0:1, 1:2], (16, 128))
    second = jnp.broadcast_to(left_where[1:2, 1:2], (16, 128))
    at = jnp.where(lane < BS, first, second) - base
    out[BS:, :] = at.astype(jnp.float32).astype(jnp.bfloat16)


def pack_left(left, left_where):
    vmem = pl.BlockSpec(memory_space=pltpu.VMEM)
    return pl.pallas_call(
        pack_left_kernel,
        out_shape=jax.ShapeDtypeStruct((LMSG, 128), jnp.bfloat16),
        in_specs=[vmem] * 2,
        out_specs=vmem,
        cost_estimate=pl.CostEstimate(flops=0, bytes_accessed=1 << 16, transcendentals=0),
    )(left, left_where)


def pack_kernel(right, right_where, pair, out, rows, tail):
    y = lax.axis_index("yh") * 2 + lax.axis_index("yl")
    core = lax.axis_index("core")
    col = lax.axis_index("col")
    base = lax.axis_index("layer") * (NB // N_LAYER)
    for p in range(PAIRS):
        both = jnp.concatenate([right[p], right[p + PAIRS]], axis=-1)
        for q in range(N_YH):
            out[q, p * BS : (p + 1) * BS, :] = both
    tail[...] = jnp.zeros_like(tail)
    inner = right_where[0:1, :] - (base + (y * 2 + core) * INNER)
    column = right_where[1:2, :] - col * COLUMNS
    tail[0:1, 0:SLOTS] = inner.astype(jnp.float32)
    tail[1:2, 0:SLOTS] = column.astype(jnp.float32)
    for q in range(N_YH):
        out[q, BODY:MSG, :] = tail[...].astype(jnp.bfloat16)
    for m in range(2):
        rows[m * BS : (m + 1) * BS, :] = pair[m, :BS, :]
    first = lax.broadcasted_iota(jnp.int32, (16, 128), 0) == 0
    marks = jnp.where(first, pair[0, BS:, :].astype(jnp.float32), pair[1, BS:, :].astype(jnp.float32))
    rows[2 * BS :, :] = marks.astype(jnp.bfloat16)


def pack(right, right_where, pair):
    vmem = pl.BlockSpec(memory_space=pltpu.VMEM)
    return pl.pallas_call(
        pack_kernel,
        out_shape=(
            jax.ShapeDtypeStruct((N_YH, MSG, 128), jnp.bfloat16),
            jax.ShapeDtypeStruct((2 * BS + 16, 128), jnp.bfloat16),
        ),
        in_specs=[vmem] * 3,
        out_specs=(vmem, vmem),
        scratch_shapes=[pltpu.VMEM((16, 128), jnp.float32)],
        cost_estimate=pl.CostEstimate(flops=0, bytes_accessed=2 << 20, transcendentals=0),
    )(right, right_where, pair)


def half_swap():
    to = lax.broadcasted_iota(jnp.int32, (128, 128), 1)
    frm = lax.broadcasted_iota(jnp.int32, (128, 128), 0)
    return (to == (frm + BS) % 128).astype(jnp.bfloat16)


def read_places(blocks, where, places, sem):
    for i, block in enumerate(blocks):
        tail = block[BODY:MSG, :].astype(jnp.float32).astype(jnp.int32)
        where[2 * i : 2 * i + 2, :] = tail[0:2, :]
    copy = pltpu.make_async_copy(where, places, sem)
    copy.start()
    return copy


def place_slots(blocks, first, panels, swapped, places):
    lane = lax.broadcasted_iota(jnp.int32, (BS, 128), 1)
    low = (lane < BS).astype(jnp.bfloat16)
    high = (lane >= BS).astype(jnp.bfloat16)

    def place(p, carry):
        at = pl.ds(pl.multiple_of(p * BS, BS), BS)
        for half in range(2):
            for i, block in enumerate(blocks):
                k = places[2 * (first + i), p + half * PAIRS]
                n = places[2 * (first + i) + 1, p + half * PAIRS]
                odd = n & 1
                value = jnp.where(odd == half, block[at, :], swapped[i][at, :])
                value = value * jnp.where(odd == 1, high, low)
                rows = pl.ds(pl.multiple_of(k * BS, BS), BS)
                lanes = pl.ds(pl.multiple_of((n >> 1) * 128, 128), 128)
                panels[i][rows, lanes] = panels[i][rows, lanes] + value
        return carry

    lax.fori_loop(0, PAIRS, place, 0, unroll=2)


def place_kernel(own, other, pieces, out, left, total, where, places, sem, *scratch):
    panels, swapped = scratch[:GROUP], scratch[GROUP:]
    yl = lax.axis_index("yl")
    core = lax.axis_index("core")
    blocks = [own.at[q] for q in range(N_YH)] + [other.at[q] for q in range(N_YH)]
    copy = read_places(blocks, where, places, sem)
    swap = half_swap()

    lane = lax.broadcasted_iota(jnp.int32, (BS, 128), 1)
    upper = (lane >= BS).astype(jnp.float32)
    for q in range(N_YH):
        for u in range(2):
            whole = pieces[3 * q + yl + u]
            there = jnp.dot(whole, swap, preferred_element_type=jnp.float32)
            here = whole.astype(jnp.float32)
            for m in range(2):
                rows = slice(m * BS, (m + 1) * BS)
                mark = 2 * BS + m
                for g in range(PIECE // 2):
                    want = upper + 2.0 * g
                    value = jnp.where(here[mark : mark + 1] == want, here[rows], 0.0)
                    value = value + jnp.where(there[mark : mark + 1] == want, there[rows], 0.0)
                    at_lane = q * WINDOW + (u * PIECE + 2 * g) * BS
                    left[rows, at_lane : at_lane + 128] = value.astype(jnp.bfloat16)

    for j0 in range(0, 2 * N_YH, GROUP):
        now = blocks[j0 : j0 + GROUP]
        for i, block in enumerate(now):
            panels[i][...] = jnp.zeros_like(panels[i])
            swapped[i][...] = jnp.dot(
                block[:BODY, :], swap, preferred_element_type=jnp.float32
            ).astype(jnp.bfloat16)
        if j0 == 0:
            copy.wait()
        place_slots(now, j0, panels, swapped, places)
        for i in range(len(now)):
            j = j0 + i
            side = core if j < N_YH else 1 - core
            start = (j % N_YH) * WINDOW + yl * (4 * BS) + side * DEPTH
            at = pl.ds(pl.multiple_of(start, 128), DEPTH)
            part = jnp.dot(left[:, at], panels[i][...], preferred_element_type=jnp.float32)
            total[...] = part if j == 0 else total[...] + part
    share = WIDTH // N_LAYER
    for m in range(2):
        for s in range(N_LAYER):
            out[m * N_LAYER + s] = total[m * BS : (m + 1) * BS, s * share : (s + 1) * share].astype(
                jnp.bfloat16
            )


def multiply(*operands):
    vmem = pl.BlockSpec(memory_space=pltpu.VMEM)
    return pl.pallas_call(
        place_kernel,
        out_shape=jax.ShapeDtypeStruct((2 * N_LAYER, BS, WIDTH // N_LAYER), jnp.bfloat16),
        in_specs=[vmem] * len(operands),
        out_specs=vmem,
        scratch_shapes=[
            pltpu.VMEM((2 * BS, N_YH * WINDOW), jnp.bfloat16),
            pltpu.VMEM((2 * BS, WIDTH), jnp.float32),
            pltpu.VMEM((16, 128), jnp.int32),
            pltpu.SMEM((16, 128), jnp.int32),
            pltpu.SemaphoreType.DMA,
        ]
        + [pltpu.VMEM((DEPTH, WIDTH), jnp.bfloat16)] * GROUP
        + [pltpu.VMEM((BODY, 128), jnp.bfloat16)] * GROUP,
        compiler_params=pltpu.CompilerParams(vmem_limit_bytes=24 * 1024 * 1024),
        cost_estimate=pl.CostEstimate(
            flops=2 * 128 * 3072 * 2048, bytes_accessed=4 << 20, transcendentals=0
        ),
    )(*operands)


def nothing_kernel(whole, when, out):
    pass


def after(whole, when):
    return pl.pallas_call(
        nothing_kernel,
        out_shape=jax.ShapeDtypeStruct(whole.shape, whole.dtype),
        in_specs=[pl.BlockSpec(memory_space=pl.ANY)] * 2,
        out_specs=pl.BlockSpec(memory_space=pl.ANY),
        input_output_aliases={0: 0},
    )(whole, when)


def shards(left_blocks, left_coords, right_blocks, right_coords):
    pair = lax.all_gather(pack_left(left_blocks.reshape(2, BS, BS), left_coords.reshape(2, 2)), "yl")
    mine, rows = pack(
        right_blocks.reshape(SLOTS, BS, BS), right_coords.reshape(SLOTS, 2).T, pair
    )
    own = lax.all_to_all(mine, "yh", 0, 0)
    pieces = lax.all_gather(rows, "col")
    other = lax.ppermute(after(own, pieces), "core", [(0, 1), (1, 0)])
    part = multiply(own, other, pieces)
    parts = lax.all_to_all(part, ("yl", "layer"), 0, 0)
    total = jnp.sum(parts.astype(jnp.float32), axis=0)
    return total.reshape(1, BS, COLUMNS // N_LAYER, BS)


def solution(mesh):
    grid = Mesh(mesh.devices.reshape(N_YH, 2, 2, N_COL, N_LAYER), ("yh", "yl", "core", "col", "layer"))
    row = ("yh", "yl", "core")
    return jax.shard_map(
        shards,
        mesh=grid,
        in_specs=(
            P(row, "col", "layer", None, None, None),
            P(row, "col", "layer", None, None),
            P(row, "col", "layer", None, None, None),
            P(row, "col", "layer", None, None),
        ),
        out_specs=P(row, None, ("col", "layer"), None),
        check_vma=False,
    )
```

```python
import jax
import jax.numpy as jnp
from jax import lax
from jax.experimental import pallas as pl
from jax.experimental.pallas import tpu as pltpu
from jax.sharding import Mesh
from jax.sharding import PartitionSpec as P

NB = 384
BS = 64
N_Y = 8
N_COL = 12
N_LAYER = 4
SLOTS = 32
PAIRS = SLOTS // 2
BODY = PAIRS * BS
MSG = BODY + 16
LMSG = BS + 16
INNER = 6
COLUMNS = NB // N_COL
PIECE = NB // N_LAYER // N_COL
DEPTH = INNER * BS
WIDTH = COLUMNS * BS
GROUP = 4


def pack_kernel(right, right_where, left, left_where, out, piece, tail):
    y = lax.axis_index("y")
    core = lax.axis_index("core")
    col = lax.axis_index("col")
    base = lax.axis_index("layer") * (NB // N_LAYER)
    for p in range(PAIRS):
        pair = jnp.concatenate([right[p], right[p + PAIRS]], axis=-1)
        for q in range(N_Y):
            out[q, p * BS : (p + 1) * BS, :] = pair
    tail[...] = jnp.zeros_like(tail)
    inner = right_where[0:1, :] - (base + (y * 2 + core) * INNER)
    column = right_where[1:2, :] - col * COLUMNS
    tail[0:1, 0:SLOTS] = inner.astype(jnp.float32)
    tail[1:2, 0:SLOTS] = column.astype(jnp.float32)
    for q in range(N_Y):
        out[q, BODY:MSG, :] = tail[...].astype(jnp.bfloat16)
    lane = lax.broadcasted_iota(jnp.int32, (16, 128), 1)
    first = jnp.broadcast_to(left_where[0:1, 1:2], (16, 128))
    second = jnp.broadcast_to(left_where[1:2, 1:2], (16, 128))
    at = jnp.where(lane < BS, first, second) - (base + col * PIECE)
    at = at.astype(jnp.float32).astype(jnp.bfloat16)
    pair = jnp.concatenate([left[0], left[1]], axis=-1)
    piece[:BS, :] = pair
    piece[BS:, :] = at


def pack(right, right_where, left, left_where):
    vmem = pl.BlockSpec(memory_space=pltpu.VMEM)
    return pl.pallas_call(
        pack_kernel,
        out_shape=(
            jax.ShapeDtypeStruct((N_Y, MSG, 128), jnp.bfloat16),
            jax.ShapeDtypeStruct((LMSG, 128), jnp.bfloat16),
        ),
        in_specs=[vmem] * 4,
        out_specs=(vmem, vmem),
        scratch_shapes=[pltpu.VMEM((16, 128), jnp.float32)],
        cost_estimate=pl.CostEstimate(flops=0, bytes_accessed=2 << 20, transcendentals=0),
    )(right, right_where, left, left_where)


def half_swap():
    to = lax.broadcasted_iota(jnp.int32, (128, 128), 1)
    frm = lax.broadcasted_iota(jnp.int32, (128, 128), 0)
    return (to == (frm + BS) % 128).astype(jnp.bfloat16)


def read_places(blocks, where, places, sem):
    for i, block in enumerate(blocks):
        tail = block[BODY:MSG, :].astype(jnp.float32).astype(jnp.int32)
        where[2 * i : 2 * i + 2, :] = tail[0:2, :]
    copy = pltpu.make_async_copy(where, places, sem)
    copy.start()
    return copy


def place_slots(blocks, first, panels, swapped, places):
    lane = lax.broadcasted_iota(jnp.int32, (BS, 128), 1)
    low = (lane < BS).astype(jnp.bfloat16)
    high = (lane >= BS).astype(jnp.bfloat16)

    def place(p, carry):
        at = pl.ds(pl.multiple_of(p * BS, BS), BS)
        for half in range(2):
            for i, block in enumerate(blocks):
                k = places[2 * (first + i), p + half * PAIRS]
                n = places[2 * (first + i) + 1, p + half * PAIRS]
                odd = n & 1
                value = jnp.where(odd == half, block[at, :], swapped[i][at, :])
                value = value * jnp.where(odd == 1, high, low)
                rows = pl.ds(pl.multiple_of(k * BS, BS), BS)
                lanes = pl.ds(pl.multiple_of((n >> 1) * 128, 128), 128)
                panels[i][rows, lanes] = panels[i][rows, lanes] + value
        return carry

    lax.fori_loop(0, PAIRS, place, 0, unroll=2)


def left_kernel(left_own, left_other, left):
    core = lax.axis_index("core")
    swap = half_swap()
    lane = lax.broadcasted_iota(jnp.int32, (BS, 128), 1)
    upper = (lane >= BS).astype(jnp.float32)
    for src, at in ((left_own, core), (left_other, 1 - core)):
        rows = pl.ds(pl.multiple_of(at * BS, BS), BS)
        for c in range(N_COL):
            whole = src[c]
            there = jnp.dot(whole, swap, preferred_element_type=jnp.float32)
            here = whole.astype(jnp.float32)
            for g in range(PIECE // 2):
                want = upper + 2.0 * g
                value = jnp.where(here[BS : BS + 1] == want, here[:BS], 0.0)
                value = value + jnp.where(there[BS : BS + 1] == want, there[:BS], 0.0)
                at_lane = (c * PIECE + 2 * g) * BS
                left[rows, at_lane : at_lane + 128] = value.astype(jnp.bfloat16)


def left_panel(left_own, left_other):
    vmem = pl.BlockSpec(memory_space=pltpu.VMEM)
    return pl.pallas_call(
        left_kernel,
        out_shape=jax.ShapeDtypeStruct((2 * BS, NB // N_LAYER * BS), jnp.bfloat16),
        in_specs=[vmem] * 2,
        out_specs=vmem,
        cost_estimate=pl.CostEstimate(flops=0, bytes_accessed=2 << 20, transcendentals=0),
    )(left_own, left_other)


def place_kernel(own, left, out, total, where, places, sem, *scratch):
    panels, swapped = scratch[:GROUP], scratch[GROUP:]
    core = lax.axis_index("core")
    blocks = [own.at[j] for j in range(N_Y)]
    copy = read_places(blocks, where, places, sem)
    swap = half_swap()
    for j0 in range(0, N_Y, GROUP):
        now = blocks[j0 : j0 + GROUP]
        for i, block in enumerate(now):
            panels[i][...] = jnp.zeros_like(panels[i])
            swapped[i][...] = jnp.dot(
                block[:BODY, :], swap, preferred_element_type=jnp.float32
            ).astype(jnp.bfloat16)
        if j0 == 0:
            copy.wait()
        place_slots(now, j0, panels, swapped, places)
        for i in range(len(now)):
            at = pl.ds(pl.multiple_of((2 * (j0 + i) + core) * DEPTH, 128), DEPTH)
            part = jnp.dot(left[:, at], panels[i][...], preferred_element_type=jnp.float32)
            total[...] = part if j0 + i == 0 else total[...] + part
    share = WIDTH // N_LAYER
    for m in range(2):
        for s in range(N_LAYER):
            out[m * N_LAYER + s] = total[m * BS : (m + 1) * BS, s * share : (s + 1) * share].astype(
                jnp.bfloat16
            )


def multiply(own, left):
    vmem = pl.BlockSpec(memory_space=pltpu.VMEM)
    return pl.pallas_call(
        place_kernel,
        out_shape=jax.ShapeDtypeStruct((2 * N_LAYER, BS, WIDTH // N_LAYER), jnp.bfloat16),
        in_specs=[vmem] * 2,
        out_specs=vmem,
        scratch_shapes=[
            pltpu.VMEM((2 * BS, WIDTH), jnp.float32),
            pltpu.VMEM((16, 128), jnp.int32),
            pltpu.SMEM((16, 128), jnp.int32),
            pltpu.SemaphoreType.DMA,
        ]
        + [pltpu.VMEM((DEPTH, WIDTH), jnp.bfloat16)] * GROUP
        + [pltpu.VMEM((BODY, 128), jnp.bfloat16)] * GROUP,
        compiler_params=pltpu.CompilerParams(vmem_limit_bytes=24 * 1024 * 1024),
        cost_estimate=pl.CostEstimate(
            flops=2 * 128 * 3072 * 2048, bytes_accessed=4 << 20, transcendentals=0
        ),
    )(own, left)


def shards(left_blocks, left_coords, right_blocks, right_coords):
    mine, piece = pack(
        right_blocks.reshape(SLOTS, BS, BS),
        right_coords.reshape(SLOTS, 2).T,
        left_blocks.reshape(2, BS, BS),
        left_coords.reshape(2, 2),
    )
    own = lax.all_to_all(mine, "y", 0, 0)
    pieces = lax.all_gather(piece, "col")
    pieces_other = lax.ppermute(pieces, "core", [(0, 1), (1, 0)])
    part = multiply(own, left_panel(pieces, pieces_other))
    parts = lax.all_to_all(part, ("core", "layer"), 0, 0)
    total = jnp.sum(parts.astype(jnp.float32), axis=0)
    return total.reshape(1, BS, COLUMNS // N_LAYER, BS)


def solution(mesh):
    grid = Mesh(mesh.devices.reshape(N_Y, 2, N_COL, N_LAYER), ("y", "core", "col", "layer"))
    row = ("y", "core")
    return jax.shard_map(
        shards,
        mesh=grid,
        in_specs=(
            P(row, "col", "layer", None, None, None),
            P(row, "col", "layer", None, None),
            P(row, "col", "layer", None, None, None),
            P(row, "col", "layer", None, None),
        ),
        out_specs=P(row, None, ("col", "layer"), None),
        check_vma=False,
    )
```

```python
import jax
import jax.numpy as jnp
from jax import lax
from jax.experimental import pallas as pl
from jax.experimental.pallas import tpu as pltpu
from jax.sharding import Mesh
from jax.sharding import PartitionSpec as P

NB = 384
BS = 64
N_Y = 8
N_COL = 12
N_LAYER = 4
SLOTS = 32
PAIRS = SLOTS // 2
BODY = PAIRS * BS
MSG = BODY + 16
LMSG = BS + 16
INNER = 6
COLUMNS = NB // N_COL
PIECE = NB // N_LAYER // N_COL
DEPTH = INNER * BS
WIDTH = COLUMNS * BS
STEPS = (0, 1, 1, 2, 2, 3, 3, 4)
OTHER = (0, 0, 1, 0, 1, 0, 1, 0)
GROUP = 4


def pack_kernel(right, right_where, out, tail):
    y = lax.axis_index("y")
    core = lax.axis_index("core")
    base = lax.axis_index("layer") * (NB // N_LAYER)
    for p in range(PAIRS):
        out[p * BS : (p + 1) * BS, :] = jnp.concatenate([right[p], right[p + PAIRS]], axis=-1)
    tail[...] = jnp.zeros_like(tail)
    inner = right_where[0:1, :] - (base + (y * 2 + core) * INNER)
    column = right_where[1:2, :] - lax.axis_index("col") * COLUMNS
    tail[0:1, 0:SLOTS] = inner.astype(jnp.float32)
    tail[1:2, 0:SLOTS] = column.astype(jnp.float32)
    out[BODY:MSG, :] = tail[...].astype(jnp.bfloat16)


def pack(right, right_where):
    vmem = pl.BlockSpec(memory_space=pltpu.VMEM)
    return pl.pallas_call(
        pack_kernel,
        out_shape=jax.ShapeDtypeStruct((MSG, 128), jnp.bfloat16),
        in_specs=[vmem] * 2,
        out_specs=vmem,
        scratch_shapes=[pltpu.VMEM((16, 128), jnp.float32)],
        cost_estimate=pl.CostEstimate(flops=0, bytes_accessed=1 << 20, transcendentals=0),
    )(right, right_where)


def spread_kernel(left, left_where, out):
    base = lax.axis_index("layer") * (NB // N_LAYER) + lax.axis_index("col") * PIECE
    lane = lax.broadcasted_iota(jnp.int32, (16, 128), 1)
    first = jnp.broadcast_to(left_where[0:1, 1:2], (16, 128))
    second = jnp.broadcast_to(left_where[1:2, 1:2], (16, 128))
    at = (jnp.where(lane < BS, first, second) - base).astype(jnp.float32).astype(jnp.bfloat16)
    pair = jnp.concatenate([left[0], left[1]], axis=-1)
    for c in range(N_COL):
        out[c, :BS, :] = pair
        out[c, BS:, :] = at


def spread(left, left_where):
    vmem = pl.BlockSpec(memory_space=pltpu.VMEM)
    return pl.pallas_call(
        spread_kernel,
        out_shape=jax.ShapeDtypeStruct((N_COL, LMSG, 128), jnp.bfloat16),
        in_specs=[vmem] * 2,
        out_specs=vmem,
        cost_estimate=pl.CostEstimate(flops=0, bytes_accessed=1 << 20, transcendentals=0),
    )(left, left_where)


def half_swap():
    to = lax.broadcasted_iota(jnp.int32, (128, 128), 1)
    frm = lax.broadcasted_iota(jnp.int32, (128, 128), 0)
    return (to == (frm + BS) % 128).astype(jnp.bfloat16)


def read_places(blocks, where, places, sem):
    for i, block in enumerate(blocks):
        tail = block[BODY:MSG, :].astype(jnp.float32).astype(jnp.int32)
        where[2 * i : 2 * i + 2, :] = tail[0:2, :]
    copy = pltpu.make_async_copy(where, places, sem)
    copy.start()
    return copy


def place_slots(blocks, first, panels, swapped, places):
    lane = lax.broadcasted_iota(jnp.int32, (BS, 128), 1)
    low = (lane < BS).astype(jnp.bfloat16)
    high = (lane >= BS).astype(jnp.bfloat16)

    def place(p, carry):
        at = pl.ds(pl.multiple_of(p * BS, BS), BS)
        for half in range(2):
            for i, block in enumerate(blocks):
                k = places[2 * (first + i), p + half * PAIRS]
                n = places[2 * (first + i) + 1, p + half * PAIRS]
                odd = n & 1
                value = jnp.where(odd == half, block[at, :], swapped[i][at, :])
                value = value * jnp.where(odd == 1, high, low)
                rows = pl.ds(pl.multiple_of(k * BS, BS), BS)
                lanes = pl.ds(pl.multiple_of((n >> 1) * 128, 128), 128)
                panels[i][rows, lanes] = panels[i][rows, lanes] + value
        return carry

    lax.fori_loop(0, PAIRS, place, 0, unroll=2)


def place_kernel(left_own, left_other, *refs):
    blocks, (out, left, total, where, places, sem), scratch = refs[:N_Y], refs[N_Y : N_Y + 6], refs[N_Y + 6 :]
    panels, swapped = scratch[:GROUP], scratch[GROUP:]
    y = lax.axis_index("y")
    core = lax.axis_index("core")
    copy = read_places(blocks, where, places, sem)
    swap = half_swap()

    lane = lax.broadcasted_iota(jnp.int32, (BS, 128), 1)
    upper = (lane >= BS).astype(jnp.float32)
    for src, at in ((left_own, core), (left_other, 1 - core)):
        rows = pl.ds(pl.multiple_of(at * BS, BS), BS)
        for c in range(N_COL):
            there = jnp.dot(src[c], swap, preferred_element_type=jnp.float32)
            here = src[c].astype(jnp.float32)
            for g in range(PIECE // 2):
                want = upper + 2.0 * g
                value = jnp.where(here[BS : BS + 1] == want, here[:BS], 0.0)
                value = value + jnp.where(there[BS : BS + 1] == want, there[:BS], 0.0)
                at_lane = (c * PIECE + 2 * g) * BS
                left[rows, at_lane : at_lane + 128] = value.astype(jnp.bfloat16)

    for j0 in range(0, N_Y, GROUP):
        now = blocks[j0 : j0 + GROUP]
        for i, block in enumerate(now):
            panels[i][...] = jnp.zeros_like(panels[i])
            swapped[i][...] = jnp.dot(
                block[:BODY, :], swap, preferred_element_type=jnp.float32
            ).astype(jnp.bfloat16)
        if j0 == 0:
            copy.wait()
        place_slots(now, j0, panels, swapped, places)
        for i in range(len(now)):
            steps = STEPS[j0 + i]
            chip = lax.rem(y + N_Y + jnp.where(core == 0, -steps, steps), N_Y)
            owner = chip * 2 + (1 - core if OTHER[j0 + i] else core)
            at = pl.ds(pl.multiple_of(owner * DEPTH, 128), DEPTH)
            part = jnp.dot(left[:, at], panels[i][...], preferred_element_type=jnp.float32)
            total[...] = part if j0 + i == 0 else total[...] + part
    share = WIDTH // N_LAYER
    for m in range(2):
        for s in range(N_LAYER):
            out[m * N_LAYER + s] = total[m * BS : (m + 1) * BS, s * share : (s + 1) * share].astype(
                jnp.bfloat16
            )


def multiply(*operands):
    vmem = pl.BlockSpec(memory_space=pltpu.VMEM)
    return pl.pallas_call(
        place_kernel,
        out_shape=jax.ShapeDtypeStruct((2 * N_LAYER, BS, WIDTH // N_LAYER), jnp.bfloat16),
        in_specs=[vmem] * len(operands),
        out_specs=vmem,
        scratch_shapes=[
            pltpu.VMEM((2 * BS, NB // N_LAYER * BS), jnp.bfloat16),
            pltpu.VMEM((2 * BS, WIDTH), jnp.float32),
            pltpu.VMEM((16, 128), jnp.int32),
            pltpu.SMEM((16, 128), jnp.int32),
            pltpu.SemaphoreType.DMA,
        ]
        + [pltpu.VMEM((DEPTH, WIDTH), jnp.bfloat16)] * GROUP
        + [pltpu.VMEM((BODY, 128), jnp.bfloat16)] * GROUP,
        compiler_params=pltpu.CompilerParams(vmem_limit_bytes=24 * 1024 * 1024),
        cost_estimate=pl.CostEstimate(
            flops=2 * 128 * 3072 * 2048, bytes_accessed=4 << 20, transcendentals=0
        ),
    )(*operands)


def shards(left_blocks, left_coords, right_blocks, right_coords):
    mine = pack(right_blocks.reshape(SLOTS, BS, BS), right_coords.reshape(SLOTS, 2).T)
    ring = [(2 * i + c, 2 * ((i + 1 - 2 * c) % N_Y) + c) for i in range(N_Y) for c in (0, 1)]
    cross = [(0, 1), (1, 0)]
    axes = ("y", "core")
    a = lax.ppermute(mine, axes, ring)
    b = lax.ppermute(mine, "core", cross)
    left = spread(left_blocks.reshape(2, BS, BS), left_coords.reshape(2, 2))
    pieces = lax.all_to_all(left, "col", 0, 0)
    blocks = [mine, a]
    for _ in range(3):
        b = lax.ppermute(b, axes, ring)
        a = lax.ppermute(a, axes, ring)
        blocks += [b, a]
    pieces_other = lax.ppermute(pieces, "core", cross)
    part = multiply(pieces, pieces_other, *blocks)
    parts = lax.all_to_all(part, ("core", "layer"), 0, 0)
    total = jnp.sum(parts.astype(jnp.float32), axis=0)
    return total.reshape(1, BS, COLUMNS // N_LAYER, BS)


def solution(mesh):
    grid = Mesh(mesh.devices.reshape(N_Y, 2, N_COL, N_LAYER), ("y", "core", "col", "layer"))
    row = ("y", "core")
    return jax.shard_map(
        shards,
        mesh=grid,
        in_specs=(
            P(row, "col", "layer", None, None, None),
            P(row, "col", "layer", None, None),
            P(row, "col", "layer", None, None, None),
            P(row, "col", "layer", None, None),
        ),
        out_specs=P(row, None, ("col", "layer"), None),
        check_vma=False,
    )
```

```python
import jax
import jax.numpy as jnp
from jax import lax
from jax.experimental import pallas as pl
from jax.experimental.pallas import tpu as pltpu
from jax.sharding import Mesh
from jax.sharding import PartitionSpec as P

NB = 384
BS = 64
N_Y = 8
N_COL = 12
N_LAYER = 4
SLOTS = 32
PAIRS = SLOTS // 2
BODY = PAIRS * BS
MSG = BODY + 16
LMSG = BS + 16
INNER = 6
COLUMNS = NB // N_COL
PIECE = NB // N_LAYER // N_COL
DEPTH = INNER * BS
WIDTH = COLUMNS * BS
STEPS = (0, -1, 1, -2, 2, -3, 3, 4)
GROUP = 4


def pack_kernel(right, right_where, out, tail):
    y = lax.axis_index("y")
    core = lax.axis_index("core")
    base = lax.axis_index("layer") * (NB // N_LAYER)
    for p in range(PAIRS):
        out[p * BS : (p + 1) * BS, :] = jnp.concatenate([right[p], right[p + PAIRS]], axis=-1)
    tail[...] = jnp.zeros_like(tail)
    inner = right_where[0:1, :] - (base + (y * 2 + core) * INNER)
    column = right_where[1:2, :] - lax.axis_index("col") * COLUMNS
    tail[0:1, 0:SLOTS] = inner.astype(jnp.float32)
    tail[1:2, 0:SLOTS] = column.astype(jnp.float32)
    out[BODY:MSG, :] = tail[...].astype(jnp.bfloat16)


def pack(right, right_where):
    vmem = pl.BlockSpec(memory_space=pltpu.VMEM)
    return pl.pallas_call(
        pack_kernel,
        out_shape=jax.ShapeDtypeStruct((MSG, 128), jnp.bfloat16),
        in_specs=[vmem] * 2,
        out_specs=vmem,
        scratch_shapes=[pltpu.VMEM((16, 128), jnp.float32)],
        cost_estimate=pl.CostEstimate(flops=0, bytes_accessed=1 << 20, transcendentals=0),
    )(right, right_where)


def spread_kernel(left, left_where, out):
    base = lax.axis_index("layer") * (NB // N_LAYER) + lax.axis_index("col") * PIECE
    lane = lax.broadcasted_iota(jnp.int32, (16, 128), 1)
    first = jnp.broadcast_to(left_where[0:1, 1:2], (16, 128))
    second = jnp.broadcast_to(left_where[1:2, 1:2], (16, 128))
    at = (jnp.where(lane < BS, first, second) - base).astype(jnp.float32).astype(jnp.bfloat16)
    pair = jnp.concatenate([left[0], left[1]], axis=-1)
    for c in range(N_COL):
        out[c, :BS, :] = pair
        out[c, BS:, :] = at


def spread(left, left_where):
    vmem = pl.BlockSpec(memory_space=pltpu.VMEM)
    return pl.pallas_call(
        spread_kernel,
        out_shape=jax.ShapeDtypeStruct((N_COL, LMSG, 128), jnp.bfloat16),
        in_specs=[vmem] * 2,
        out_specs=vmem,
        cost_estimate=pl.CostEstimate(flops=0, bytes_accessed=1 << 20, transcendentals=0),
    )(left, left_where)


def half_swap():
    to = lax.broadcasted_iota(jnp.int32, (128, 128), 1)
    frm = lax.broadcasted_iota(jnp.int32, (128, 128), 0)
    return (to == (frm + BS) % 128).astype(jnp.bfloat16)


def read_places(blocks, where, places, sem):
    for i, block in enumerate(blocks):
        tail = block[BODY:MSG, :].astype(jnp.float32).astype(jnp.int32)
        where[2 * i : 2 * i + 2, :] = tail[0:2, :]
    copy = pltpu.make_async_copy(where, places, sem)
    copy.start()
    return copy


def place_slots(blocks, first, panels, swapped, places):
    lane = lax.broadcasted_iota(jnp.int32, (BS, 128), 1)
    low = (lane < BS).astype(jnp.bfloat16)
    high = (lane >= BS).astype(jnp.bfloat16)

    def place(p, carry):
        at = pl.ds(pl.multiple_of(p * BS, BS), BS)
        for half in range(2):
            for i, block in enumerate(blocks):
                k = places[2 * (first + i), p + half * PAIRS]
                n = places[2 * (first + i) + 1, p + half * PAIRS]
                odd = n & 1
                value = jnp.where(odd == half, block[at, :], swapped[i][at, :])
                value = value * jnp.where(odd == 1, high, low)
                rows = pl.ds(pl.multiple_of(k * BS, BS), BS)
                lanes = pl.ds(pl.multiple_of((n >> 1) * 128, 128), 128)
                panels[i][rows, lanes] = panels[i][rows, lanes] + value
        return carry

    lax.fori_loop(0, PAIRS, place, 0, unroll=2)


def place_kernel(left_own, left_other, *refs):
    blocks, (out, left, total, where, places, sem), scratch = refs[:N_Y], refs[N_Y : N_Y + 6], refs[N_Y + 6 :]
    panels, swapped = scratch[:GROUP], scratch[GROUP:]
    y = lax.axis_index("y")
    core = lax.axis_index("core")
    copy = read_places(blocks, where, places, sem)
    swap = half_swap()

    lane = lax.broadcasted_iota(jnp.int32, (BS, 128), 1)
    upper = (lane >= BS).astype(jnp.float32)
    for src, at in ((left_own, core), (left_other, 1 - core)):
        rows = pl.ds(pl.multiple_of(at * BS, BS), BS)
        for c in range(N_COL):
            there = jnp.dot(src[c], swap, preferred_element_type=jnp.float32)
            here = src[c].astype(jnp.float32)
            for g in range(PIECE // 2):
                want = upper + 2.0 * g
                value = jnp.where(here[BS : BS + 1] == want, here[:BS], 0.0)
                value = value + jnp.where(there[BS : BS + 1] == want, there[:BS], 0.0)
                at_lane = (c * PIECE + 2 * g) * BS
                left[rows, at_lane : at_lane + 128] = value.astype(jnp.bfloat16)

    for j0 in range(0, N_Y, GROUP):
        now = blocks[j0 : j0 + GROUP]
        for i, block in enumerate(now):
            panels[i][...] = jnp.zeros_like(panels[i])
            swapped[i][...] = jnp.dot(
                block[:BODY, :], swap, preferred_element_type=jnp.float32
            ).astype(jnp.bfloat16)
        if j0 == 0:
            copy.wait()
        place_slots(now, j0, panels, swapped, places)
        for i in range(len(now)):
            chip = lax.rem(y + N_Y + STEPS[j0 + i], N_Y)
            at = pl.ds(pl.multiple_of((2 * chip + core) * DEPTH, 128), DEPTH)
            part = jnp.dot(left[:, at], panels[i][...], preferred_element_type=jnp.float32)
            total[...] = part if j0 + i == 0 else total[...] + part
    share = WIDTH // N_LAYER
    for m in range(2):
        for s in range(N_LAYER):
            out[m * N_LAYER + s] = total[m * BS : (m + 1) * BS, s * share : (s + 1) * share].astype(
                jnp.bfloat16
            )


def multiply(*operands):
    vmem = pl.BlockSpec(memory_space=pltpu.VMEM)
    return pl.pallas_call(
        place_kernel,
        out_shape=jax.ShapeDtypeStruct((2 * N_LAYER, BS, WIDTH // N_LAYER), jnp.bfloat16),
        in_specs=[vmem] * len(operands),
        out_specs=vmem,
        scratch_shapes=[
            pltpu.VMEM((2 * BS, NB // N_LAYER * BS), jnp.bfloat16),
            pltpu.VMEM((2 * BS, WIDTH), jnp.float32),
            pltpu.VMEM((16, 128), jnp.int32),
            pltpu.SMEM((16, 128), jnp.int32),
            pltpu.SemaphoreType.DMA,
        ]
        + [pltpu.VMEM((DEPTH, WIDTH), jnp.bfloat16)] * GROUP
        + [pltpu.VMEM((BODY, 128), jnp.bfloat16)] * GROUP,
        compiler_params=pltpu.CompilerParams(vmem_limit_bytes=24 * 1024 * 1024),
        cost_estimate=pl.CostEstimate(
            flops=2 * 128 * 3072 * 2048, bytes_accessed=4 << 20, transcendentals=0
        ),
    )(*operands)


def shards(left_blocks, left_coords, right_blocks, right_coords):
    mine = pack(right_blocks.reshape(SLOTS, BS, BS), right_coords.reshape(SLOTS, 2).T)
    cross = [(0, 1), (1, 0)]
    away = {d: [(i, (i + d) % N_Y) for i in range(N_Y)] for d in (-2, -1, 1, 2)}
    far = [(2 * i + c, 2 * ((i + 2 - 4 * c) % N_Y) + c) for i in range(N_Y) for c in (0, 1)]
    one = [lax.ppermute(mine, "y", away[d]) for d in (1, -1)]
    two = [lax.ppermute(mine, "y", away[d]) for d in (2, -2)]
    left = spread(left_blocks.reshape(2, BS, BS), left_coords.reshape(2, 2))
    pieces = lax.all_to_all(left, "col", 0, 0)
    three = [lax.ppermute(two[0], "y", away[1]), lax.ppermute(two[1], "y", away[-1])]
    four = lax.ppermute(jnp.where(lax.axis_index("core") == 0, *two), ("y", "core"), far)
    blocks = [mine, *one, *two, *three, four]
    pieces_other = lax.ppermute(pieces, "core", cross)
    part = multiply(pieces, pieces_other, *blocks)
    parts = lax.all_to_all(part, ("core", "layer"), 0, 0)
    total = jnp.sum(parts.astype(jnp.float32), axis=0)
    return total.reshape(1, BS, COLUMNS // N_LAYER, BS)


def solution(mesh):
    grid = Mesh(mesh.devices.reshape(N_Y, 2, N_COL, N_LAYER), ("y", "core", "col", "layer"))
    row = ("y", "core")
    return jax.shard_map(
        shards,
        mesh=grid,
        in_specs=(
            P(row, "col", "layer", None, None, None),
            P(row, "col", "layer", None, None),
            P(row, "col", "layer", None, None, None),
            P(row, "col", "layer", None, None),
        ),
        out_specs=P(row, None, ("col", "layer"), None),
        check_vma=False,
    )
```

```python
import jax
import jax.numpy as jnp
from jax import lax
from jax.experimental import pallas as pl
from jax.experimental.pallas import tpu as pltpu
from jax.sharding import Mesh
from jax.sharding import PartitionSpec as P

NB = 384
BS = 64
N_YH = 4
N_COL = 12
N_LAYER = 4
SLOTS = 32
PAIRS = SLOTS // 2
BODY = PAIRS * BS
MSG = BODY + 16
LMSG = BS + 16
INNER = 6
COLUMNS = NB // N_COL
PIECE = NB // N_LAYER // N_COL
DEPTH = INNER * BS
WIDTH = COLUMNS * BS
GROUP = 4
WINDOW = 2 * PIECE * BS
AWAY = (0, 3, 1, 2)


def pack_kernel(right, right_where, out, tail):
    y = lax.axis_index("yh") * 2 + lax.axis_index("yl")
    core = lax.axis_index("core")
    base = lax.axis_index("layer") * (NB // N_LAYER)
    for p in range(PAIRS):
        out[p * BS : (p + 1) * BS, :] = jnp.concatenate([right[p], right[p + PAIRS]], axis=-1)
    tail[...] = jnp.zeros_like(tail)
    inner = right_where[0:1, :] - (base + (y * 2 + core) * INNER)
    column = right_where[1:2, :] - lax.axis_index("col") * COLUMNS
    tail[0:1, 0:SLOTS] = inner.astype(jnp.float32)
    tail[1:2, 0:SLOTS] = column.astype(jnp.float32)
    out[BODY:MSG, :] = tail[...].astype(jnp.bfloat16)


def pack(right, right_where):
    vmem = pl.BlockSpec(memory_space=pltpu.VMEM)
    return pl.pallas_call(
        pack_kernel,
        out_shape=jax.ShapeDtypeStruct((MSG, 128), jnp.bfloat16),
        in_specs=[vmem] * 2,
        out_specs=vmem,
        scratch_shapes=[pltpu.VMEM((16, 128), jnp.float32)],
        cost_estimate=pl.CostEstimate(flops=0, bytes_accessed=1 << 20, transcendentals=0),
    )(right, right_where)


def spread_kernel(left, left_where, out):
    base = lax.axis_index("layer") * (NB // N_LAYER) + lax.axis_index("col") * PIECE
    lane = lax.broadcasted_iota(jnp.int32, (16, 128), 1)
    first = jnp.broadcast_to(left_where[0:1, 1:2], (16, 128))
    second = jnp.broadcast_to(left_where[1:2, 1:2], (16, 128))
    at = (jnp.where(lane < BS, first, second) - base).astype(jnp.float32).astype(jnp.bfloat16)
    pair = jnp.concatenate([left[0], left[1]], axis=-1)
    for c in range(N_COL):
        out[c, :BS, :] = pair
        out[c, BS:, :] = at


def spread(left, left_where):
    vmem = pl.BlockSpec(memory_space=pltpu.VMEM)
    return pl.pallas_call(
        spread_kernel,
        out_shape=jax.ShapeDtypeStruct((N_COL, LMSG, 128), jnp.bfloat16),
        in_specs=[vmem] * 2,
        out_specs=vmem,
        cost_estimate=pl.CostEstimate(flops=0, bytes_accessed=1 << 20, transcendentals=0),
    )(left, left_where)


def half_swap():
    to = lax.broadcasted_iota(jnp.int32, (128, 128), 1)
    frm = lax.broadcasted_iota(jnp.int32, (128, 128), 0)
    return (to == (frm + BS) % 128).astype(jnp.bfloat16)


def read_places(blocks, where, places, sem):
    for i, block in enumerate(blocks):
        tail = block[BODY:MSG, :].astype(jnp.float32).astype(jnp.int32)
        where[2 * i : 2 * i + 2, :] = tail[0:2, :]
    copy = pltpu.make_async_copy(where, places, sem)
    copy.start()
    return copy


def place_slots(blocks, first, panels, swapped, places):
    lane = lax.broadcasted_iota(jnp.int32, (BS, 128), 1)
    low = (lane < BS).astype(jnp.bfloat16)
    high = (lane >= BS).astype(jnp.bfloat16)

    def place(p, carry):
        at = pl.ds(pl.multiple_of(p * BS, BS), BS)
        for half in range(2):
            for i, block in enumerate(blocks):
                k = places[2 * (first + i), p + half * PAIRS]
                n = places[2 * (first + i) + 1, p + half * PAIRS]
                odd = n & 1
                value = jnp.where(odd == half, block[at, :], swapped[i][at, :])
                value = value * jnp.where(odd == 1, high, low)
                rows = pl.ds(pl.multiple_of(k * BS, BS), BS)
                lanes = pl.ds(pl.multiple_of((n >> 1) * 128, 128), 128)
                panels[i][rows, lanes] = panels[i][rows, lanes] + value
        return carry

    lax.fori_loop(0, PAIRS, place, 0, unroll=2)


def place_kernel(left_own, left_other, mine, below, above, far, others, last, *refs):
    (out, left, total, where, places, sem), scratch = refs[:6], refs[6:]
    panels, swapped = scratch[:GROUP], scratch[GROUP:]
    blocks = [mine, below, above, far, others.at[0], last, others.at[1], others.at[2]]
    yh = lax.axis_index("yh")
    yl = lax.axis_index("yl")
    core = lax.axis_index("core")
    copy = read_places(blocks, where, places, sem)
    swap = half_swap()

    lane = lax.broadcasted_iota(jnp.int32, (BS, 128), 1)
    upper = (lane >= BS).astype(jnp.float32)
    for src, at in ((left_own, yl), (left_other, 1 - yl)):
        rows = pl.ds(pl.multiple_of(at * BS, BS), BS)
        for q in range(N_YH):
            for u in range(2):
                whole = src[3 * q + yl + u] if src is left_own else src[2 * q + u]
                there = jnp.dot(whole, swap, preferred_element_type=jnp.float32)
                here = whole.astype(jnp.float32)
                for g in range(PIECE // 2):
                    want = upper + 2.0 * g
                    value = jnp.where(here[BS : BS + 1] == want, here[:BS], 0.0)
                    value = value + jnp.where(there[BS : BS + 1] == want, there[:BS], 0.0)
                    at_lane = q * WINDOW + (u * PIECE + 2 * g) * BS
                    left[rows, at_lane : at_lane + 128] = value.astype(jnp.bfloat16)

    for j0 in range(0, 2 * N_YH, GROUP):
        now = blocks[j0 : j0 + GROUP]
        for i, block in enumerate(now):
            panels[i][...] = jnp.zeros_like(panels[i])
            swapped[i][...] = jnp.dot(
                block[:BODY, :], swap, preferred_element_type=jnp.float32
            ).astype(jnp.bfloat16)
        if j0 == 0:
            copy.wait()
        place_slots(now, j0, panels, swapped, places)
        for i in range(len(now)):
            j = j0 + i
            side = core if j < N_YH else 1 - core
            window = lax.rem(yh + AWAY[j % N_YH], N_YH)
            start = window * WINDOW + yl * (4 * BS) + side * DEPTH
            at = pl.ds(pl.multiple_of(start, 128), DEPTH)
            part = jnp.dot(left[:, at], panels[i][...], preferred_element_type=jnp.float32)
            total[...] = part if j0 + i == 0 else total[...] + part
    share = WIDTH // N_LAYER
    for m in range(2):
        for s in range(N_LAYER):
            out[m * N_LAYER + s] = total[m * BS : (m + 1) * BS, s * share : (s + 1) * share].astype(
                jnp.bfloat16
            )


def multiply(*operands):
    vmem = pl.BlockSpec(memory_space=pltpu.VMEM)
    return pl.pallas_call(
        place_kernel,
        out_shape=jax.ShapeDtypeStruct((2 * N_LAYER, BS, WIDTH // N_LAYER), jnp.bfloat16),
        in_specs=[vmem] * len(operands),
        out_specs=vmem,
        scratch_shapes=[
            pltpu.VMEM((2 * BS, N_YH * WINDOW), jnp.bfloat16),
            pltpu.VMEM((2 * BS, WIDTH), jnp.float32),
            pltpu.VMEM((16, 128), jnp.int32),
            pltpu.SMEM((16, 128), jnp.int32),
            pltpu.SemaphoreType.DMA,
        ]
        + [pltpu.VMEM((DEPTH, WIDTH), jnp.bfloat16)] * GROUP
        + [pltpu.VMEM((BODY, 128), jnp.bfloat16)] * GROUP,
        compiler_params=pltpu.CompilerParams(vmem_limit_bytes=24 * 1024 * 1024),
        cost_estimate=pl.CostEstimate(
            flops=2 * 128 * 3072 * 2048, bytes_accessed=4 << 20, transcendentals=0
        ),
    )(*operands)


def shards(left_blocks, left_coords, right_blocks, right_coords):
    mine = pack(right_blocks.reshape(SLOTS, BS, BS), right_coords.reshape(SLOTS, 2).T)
    yl = lax.axis_index("yl")
    cross = [(0, 1), (1, 0)]
    below, far, above = (
        lax.ppermute(mine, "yh", [(i, (i + d) % N_YH) for i in range(N_YH)]) for d in (1, 2, 3)
    )
    left = spread(left_blocks.reshape(2, BS, BS), left_coords.reshape(2, 2))
    pieces = lax.all_to_all(left, "col", 0, 0)
    others = lax.ppermute(jnp.stack([mine, above, far]), "core", cross)
    last = lax.ppermute(below, "core", cross)
    wanted = lax.dynamic_slice_in_dim(pieces.reshape(N_YH, 3, LMSG, 128), 1 - yl, 2, 1)
    pieces_other = lax.ppermute(wanted.reshape(2 * N_YH, LMSG, 128), "yl", cross)
    part = multiply(pieces, pieces_other, mine, below, above, far, others, last)
    parts = lax.all_to_all(part, ("yl", "layer"), 0, 0)
    total = jnp.sum(parts.astype(jnp.float32), axis=0)
    return total.reshape(1, BS, COLUMNS // N_LAYER, BS)


def solution(mesh):
    grid = Mesh(mesh.devices.reshape(N_YH, 2, 2, N_COL, N_LAYER), ("yh", "yl", "core", "col", "layer"))
    row = ("yh", "yl", "core")
    return jax.shard_map(
        shards,
        mesh=grid,
        in_specs=(
            P(row, "col", "layer", None, None, None),
            P(row, "col", "layer", None, None),
            P(row, "col", "layer", None, None, None),
            P(row, "col", "layer", None, None),
        ),
        out_specs=P(row, None, ("col", "layer"), None),
        check_vma=False,
    )
```

```python
import jax
import jax.numpy as jnp
from jax import lax
from jax.experimental import pallas as pl
from jax.experimental.pallas import tpu as pltpu
from jax.sharding import Mesh
from jax.sharding import PartitionSpec as P

NB = 384
BS = 64
N_Y = 8
N_COL = 12
N_LAYER = 4
SLOTS = 32
PAIRS = SLOTS // 2
BODY = PAIRS * BS
MSG = BODY + 16
LMSG = BS + 16
INNER = 6
COLUMNS = NB // N_COL
PIECE = NB // N_LAYER // N_COL
DEPTH = INNER * BS
WIDTH = COLUMNS * BS
STEPS = (0, 1, 1, 2, 2, 3, 3, 4)
OTHER = (0, 0, 1, 0, 1, 0, 1, 0)
GROUP = 4


def pack_kernel(right, right_where, out, tail):
    y = lax.axis_index("y")
    core = lax.axis_index("core")
    base = lax.axis_index("layer") * (NB // N_LAYER)
    for p in range(PAIRS):
        out[p * BS : (p + 1) * BS, :] = jnp.concatenate([right[p], right[p + PAIRS]], axis=-1)
    tail[...] = jnp.zeros_like(tail)
    inner = right_where[0:1, :] - (base + (y * 2 + core) * INNER)
    column = right_where[1:2, :] - lax.axis_index("col") * COLUMNS
    tail[0:1, 0:SLOTS] = inner.astype(jnp.float32)
    tail[1:2, 0:SLOTS] = column.astype(jnp.float32)
    out[BODY:MSG, :] = tail[...].astype(jnp.bfloat16)


def pack(right, right_where):
    vmem = pl.BlockSpec(memory_space=pltpu.VMEM)
    return pl.pallas_call(
        pack_kernel,
        out_shape=jax.ShapeDtypeStruct((MSG, 128), jnp.bfloat16),
        in_specs=[vmem] * 2,
        out_specs=vmem,
        scratch_shapes=[pltpu.VMEM((16, 128), jnp.float32)],
        cost_estimate=pl.CostEstimate(flops=0, bytes_accessed=1 << 20, transcendentals=0),
    )(right, right_where)


def spread_kernel(left, left_where, out):
    base = lax.axis_index("layer") * (NB // N_LAYER) + lax.axis_index("col") * PIECE
    lane = lax.broadcasted_iota(jnp.int32, (16, 128), 1)
    first = jnp.broadcast_to(left_where[0:1, 1:2], (16, 128))
    second = jnp.broadcast_to(left_where[1:2, 1:2], (16, 128))
    at = (jnp.where(lane < BS, first, second) - base).astype(jnp.float32).astype(jnp.bfloat16)
    pair = jnp.concatenate([left[0], left[1]], axis=-1)
    for c in range(N_COL):
        out[c, :BS, :] = pair
        out[c, BS:, :] = at


def spread(left, left_where):
    vmem = pl.BlockSpec(memory_space=pltpu.VMEM)
    return pl.pallas_call(
        spread_kernel,
        out_shape=jax.ShapeDtypeStruct((N_COL, LMSG, 128), jnp.bfloat16),
        in_specs=[vmem] * 2,
        out_specs=vmem,
        cost_estimate=pl.CostEstimate(flops=0, bytes_accessed=1 << 20, transcendentals=0),
    )(left, left_where)


def half_swap():
    to = lax.broadcasted_iota(jnp.int32, (128, 128), 1)
    frm = lax.broadcasted_iota(jnp.int32, (128, 128), 0)
    return (to == (frm + BS) % 128).astype(jnp.bfloat16)


def read_places(blocks, where, places, sem):
    for i, block in enumerate(blocks):
        tail = block[BODY:MSG, :].astype(jnp.float32).astype(jnp.int32)
        where[2 * i : 2 * i + 2, :] = tail[0:2, :]
    copy = pltpu.make_async_copy(where, places, sem)
    copy.start()
    return copy


def place_slots(blocks, first, panels, swapped, places):
    lane = lax.broadcasted_iota(jnp.int32, (BS, 128), 1)
    low = (lane < BS).astype(jnp.bfloat16)
    high = (lane >= BS).astype(jnp.bfloat16)

    def place(p, carry):
        at = pl.ds(pl.multiple_of(p * BS, BS), BS)
        for half in range(2):
            for i, block in enumerate(blocks):
                k = places[2 * (first + i), p + half * PAIRS]
                n = places[2 * (first + i) + 1, p + half * PAIRS]
                odd = n & 1
                value = jnp.where(odd == half, block[at, :], swapped[i][at, :])
                value = value * jnp.where(odd == 1, high, low)
                rows = pl.ds(pl.multiple_of(k * BS, BS), BS)
                lanes = pl.ds(pl.multiple_of((n >> 1) * 128, 128), 128)
                panels[i][rows, lanes] = panels[i][rows, lanes] + value
        return carry

    lax.fori_loop(0, PAIRS, place, 0, unroll=2)


def place_kernel(left_own, left_other, mine, one, two, three, four, *refs):
    (out, left, total, where, places, sem), scratch = refs[:6], refs[6:]
    blocks = [mine, one.at[0], one.at[1], two.at[0], two.at[1], three.at[0], three.at[1], four]
    panels, swapped = scratch[:GROUP], scratch[GROUP:]
    y = lax.axis_index("y")
    core = lax.axis_index("core")
    copy = read_places(blocks, where, places, sem)
    swap = half_swap()

    lane = lax.broadcasted_iota(jnp.int32, (BS, 128), 1)
    upper = (lane >= BS).astype(jnp.float32)
    for src, at in ((left_own, core), (left_other, 1 - core)):
        rows = pl.ds(pl.multiple_of(at * BS, BS), BS)
        for c in range(N_COL):
            there = jnp.dot(src[c], swap, preferred_element_type=jnp.float32)
            here = src[c].astype(jnp.float32)
            for g in range(PIECE // 2):
                want = upper + 2.0 * g
                value = jnp.where(here[BS : BS + 1] == want, here[:BS], 0.0)
                value = value + jnp.where(there[BS : BS + 1] == want, there[:BS], 0.0)
                at_lane = (c * PIECE + 2 * g) * BS
                left[rows, at_lane : at_lane + 128] = value.astype(jnp.bfloat16)

    for j0 in range(0, N_Y, GROUP):
        now = blocks[j0 : j0 + GROUP]
        for i, block in enumerate(now):
            panels[i][...] = jnp.zeros_like(panels[i])
            swapped[i][...] = jnp.dot(
                block[:BODY, :], swap, preferred_element_type=jnp.float32
            ).astype(jnp.bfloat16)
        if j0 == 0:
            copy.wait()
        place_slots(now, j0, panels, swapped, places)
        for i in range(len(now)):
            steps = STEPS[j0 + i]
            chip = lax.rem(y + N_Y + jnp.where(core == 0, -steps, steps), N_Y)
            owner = chip * 2 + (1 - core if OTHER[j0 + i] else core)
            at = pl.ds(pl.multiple_of(owner * DEPTH, 128), DEPTH)
            part = jnp.dot(left[:, at], panels[i][...], preferred_element_type=jnp.float32)
            total[...] = part if j0 + i == 0 else total[...] + part
    share = WIDTH // N_LAYER
    for m in range(2):
        for s in range(N_LAYER):
            out[m * N_LAYER + s] = total[m * BS : (m + 1) * BS, s * share : (s + 1) * share].astype(
                jnp.bfloat16
            )


def multiply(*operands):
    vmem = pl.BlockSpec(memory_space=pltpu.VMEM)
    return pl.pallas_call(
        place_kernel,
        out_shape=jax.ShapeDtypeStruct((2 * N_LAYER, BS, WIDTH // N_LAYER), jnp.bfloat16),
        in_specs=[vmem] * len(operands),
        out_specs=vmem,
        scratch_shapes=[
            pltpu.VMEM((2 * BS, NB // N_LAYER * BS), jnp.bfloat16),
            pltpu.VMEM((2 * BS, WIDTH), jnp.float32),
            pltpu.VMEM((16, 128), jnp.int32),
            pltpu.SMEM((16, 128), jnp.int32),
            pltpu.SemaphoreType.DMA,
        ]
        + [pltpu.VMEM((DEPTH, WIDTH), jnp.bfloat16)] * GROUP
        + [pltpu.VMEM((BODY, 128), jnp.bfloat16)] * GROUP,
        compiler_params=pltpu.CompilerParams(vmem_limit_bytes=24 * 1024 * 1024),
        cost_estimate=pl.CostEstimate(
            flops=2 * 128 * 3072 * 2048, bytes_accessed=4 << 20, transcendentals=0
        ),
    )(*operands)


def shards(left_blocks, left_coords, right_blocks, right_coords):
    mine = pack(right_blocks.reshape(SLOTS, BS, BS), right_coords.reshape(SLOTS, 2).T)
    cross = [(0, 1), (1, 0)]
    on = [
        [(2 * i + c, 2 * ((i + d * (1 - 2 * c)) % N_Y) + c) for i in range(N_Y) for c in (0, 1)]
        for d in range(3)
    ]
    axes = ("y", "core")
    both = jnp.stack([mine, lax.ppermute(mine, "core", cross)])
    one = lax.ppermute(both, axes, on[1])
    two = lax.ppermute(both, axes, on[2])
    left = spread(left_blocks.reshape(2, BS, BS), left_coords.reshape(2, 2))
    pieces = lax.all_to_all(left, "col", 0, 0)
    three = lax.ppermute(two, axes, on[1])
    four = lax.ppermute(two[0], axes, on[2])
    blocks = [mine, one, two, three, four]
    pieces_other = lax.ppermute(pieces, "core", cross)
    part = multiply(pieces, pieces_other, *blocks)
    parts = lax.all_to_all(part, ("core", "layer"), 0, 0)
    total = jnp.sum(parts.astype(jnp.float32), axis=0)
    return total.reshape(1, BS, COLUMNS // N_LAYER, BS)


def solution(mesh):
    grid = Mesh(mesh.devices.reshape(N_Y, 2, N_COL, N_LAYER), ("y", "core", "col", "layer"))
    row = ("y", "core")
    return jax.shard_map(
        shards,
        mesh=grid,
        in_specs=(
            P(row, "col", "layer", None, None, None),
            P(row, "col", "layer", None, None),
            P(row, "col", "layer", None, None, None),
            P(row, "col", "layer", None, None),
        ),
        out_specs=P(row, None, ("col", "layer"), None),
        check_vma=False,
    )
```

```python
import jax
import jax.numpy as jnp
from jax import lax
from jax.experimental import pallas as pl
from jax.experimental.pallas import tpu as pltpu
from jax.sharding import Mesh
from jax.sharding import PartitionSpec as P

NB = 384
BS = 64
N_Y = 8
N_COL = 12
N_LAYER = 4
SLOTS = 32
PAIRS = SLOTS // 2
BODY = PAIRS * BS
MSG = BODY + 16
LMSG = BS + 16
INNER = 6
COLUMNS = NB // N_COL
PIECE = NB // N_LAYER // N_COL
DEPTH = INNER * BS
WIDTH = COLUMNS * BS
STEPS = (0, 1, 1, 2, 2, 3, 3, 4)
OTHER = (0, 0, 1, 0, 1, 0, 1, 0)
GROUP = 4


def pack_kernel(right, right_where, out, tail):
    y = lax.axis_index("y")
    core = lax.axis_index("core")
    base = lax.axis_index("layer") * (NB // N_LAYER)
    for p in range(PAIRS):
        out[p * BS : (p + 1) * BS, :] = jnp.concatenate([right[p], right[p + PAIRS]], axis=-1)
    tail[...] = jnp.zeros_like(tail)
    inner = right_where[0:1, :] - (base + (y * 2 + core) * INNER)
    column = right_where[1:2, :] - lax.axis_index("col") * COLUMNS
    tail[0:1, 0:SLOTS] = inner.astype(jnp.float32)
    tail[1:2, 0:SLOTS] = column.astype(jnp.float32)
    out[BODY:MSG, :] = tail[...].astype(jnp.bfloat16)


def pack(right, right_where):
    vmem = pl.BlockSpec(memory_space=pltpu.VMEM)
    return pl.pallas_call(
        pack_kernel,
        out_shape=jax.ShapeDtypeStruct((MSG, 128), jnp.bfloat16),
        in_specs=[vmem] * 2,
        out_specs=vmem,
        scratch_shapes=[pltpu.VMEM((16, 128), jnp.float32)],
        cost_estimate=pl.CostEstimate(flops=0, bytes_accessed=1 << 20, transcendentals=0),
    )(right, right_where)


def spread_kernel(left, left_where, out):
    base = lax.axis_index("layer") * (NB // N_LAYER) + lax.axis_index("col") * PIECE
    lane = lax.broadcasted_iota(jnp.int32, (16, 128), 1)
    first = jnp.broadcast_to(left_where[0:1, 1:2], (16, 128))
    second = jnp.broadcast_to(left_where[1:2, 1:2], (16, 128))
    at = (jnp.where(lane < BS, first, second) - base).astype(jnp.float32).astype(jnp.bfloat16)
    pair = jnp.concatenate([left[0], left[1]], axis=-1)
    for c in range(N_COL):
        out[c, :BS, :] = pair
        out[c, BS:, :] = at


def spread(left, left_where):
    vmem = pl.BlockSpec(memory_space=pltpu.VMEM)
    return pl.pallas_call(
        spread_kernel,
        out_shape=jax.ShapeDtypeStruct((N_COL, LMSG, 128), jnp.bfloat16),
        in_specs=[vmem] * 2,
        out_specs=vmem,
        cost_estimate=pl.CostEstimate(flops=0, bytes_accessed=1 << 20, transcendentals=0),
    )(left, left_where)


def half_swap():
    to = lax.broadcasted_iota(jnp.int32, (128, 128), 1)
    frm = lax.broadcasted_iota(jnp.int32, (128, 128), 0)
    return (to == (frm + BS) % 128).astype(jnp.bfloat16)


def read_places(blocks, where, places, sem):
    for i, block in enumerate(blocks):
        tail = block[BODY:MSG, :].astype(jnp.float32).astype(jnp.int32)
        where[2 * i : 2 * i + 2, :] = tail[0:2, :]
    copy = pltpu.make_async_copy(where, places, sem)
    copy.start()
    return copy


def place_slots(blocks, first, panels, swapped, places):
    lane = lax.broadcasted_iota(jnp.int32, (BS, 128), 1)
    low = (lane < BS).astype(jnp.bfloat16)
    high = (lane >= BS).astype(jnp.bfloat16)

    def place(p, carry):
        at = pl.ds(pl.multiple_of(p * BS, BS), BS)
        for half in range(2):
            for i, block in enumerate(blocks):
                k = places[2 * (first + i), p + half * PAIRS]
                n = places[2 * (first + i) + 1, p + half * PAIRS]
                odd = n & 1
                value = jnp.where(odd == half, block[at, :], swapped[i][at, :])
                value = value * jnp.where(odd == 1, high, low)
                rows = pl.ds(pl.multiple_of(k * BS, BS), BS)
                lanes = pl.ds(pl.multiple_of((n >> 1) * 128, 128), 128)
                panels[i][rows, lanes] = panels[i][rows, lanes] + value
        return carry

    lax.fori_loop(0, PAIRS, place, 0, unroll=2)


def place_kernel(left_own, left_other, mine, one, two, three, four, *refs):
    (out, left, total, where, places, sem), scratch = refs[:6], refs[6:]
    blocks = [mine, one.at[0], one.at[1], two.at[0], two.at[1], three.at[0], three.at[1], four]
    panels, swapped = scratch[:GROUP], scratch[GROUP:]
    y = lax.axis_index("y")
    core = lax.axis_index("core")
    copy = read_places(blocks, where, places, sem)
    swap = half_swap()

    lane = lax.broadcasted_iota(jnp.int32, (BS, 128), 1)
    upper = (lane >= BS).astype(jnp.float32)
    for src, at in ((left_own, core), (left_other, 1 - core)):
        rows = pl.ds(pl.multiple_of(at * BS, BS), BS)
        for c in range(N_COL):
            there = jnp.dot(src[c], swap, preferred_element_type=jnp.float32)
            here = src[c].astype(jnp.float32)
            for g in range(PIECE // 2):
                want = upper + 2.0 * g
                value = jnp.where(here[BS : BS + 1] == want, here[:BS], 0.0)
                value = value + jnp.where(there[BS : BS + 1] == want, there[:BS], 0.0)
                at_lane = (c * PIECE + 2 * g) * BS
                left[rows, at_lane : at_lane + 128] = value.astype(jnp.bfloat16)

    for j0 in range(0, N_Y, GROUP):
        now = blocks[j0 : j0 + GROUP]
        for i, block in enumerate(now):
            panels[i][...] = jnp.zeros_like(panels[i])
            swapped[i][...] = jnp.dot(
                block[:BODY, :], swap, preferred_element_type=jnp.float32
            ).astype(jnp.bfloat16)
        if j0 == 0:
            copy.wait()
        place_slots(now, j0, panels, swapped, places)
        for i in range(len(now)):
            steps = STEPS[j0 + i]
            chip = lax.rem(y + N_Y + jnp.where(core == 0, -steps, steps), N_Y)
            owner = chip * 2 + (1 - core if OTHER[j0 + i] else core)
            at = pl.ds(pl.multiple_of(owner * DEPTH, 128), DEPTH)
            part = jnp.dot(left[:, at], panels[i][...], preferred_element_type=jnp.float32)
            total[...] = part if j0 + i == 0 else total[...] + part
    share = WIDTH // N_LAYER
    for m in range(2):
        for s in range(N_LAYER):
            out[m * N_LAYER + s] = total[m * BS : (m + 1) * BS, s * share : (s + 1) * share].astype(
                jnp.bfloat16
            )


def multiply(*operands):
    vmem = pl.BlockSpec(memory_space=pltpu.VMEM)
    return pl.pallas_call(
        place_kernel,
        out_shape=jax.ShapeDtypeStruct((2 * N_LAYER, BS, WIDTH // N_LAYER), jnp.bfloat16),
        in_specs=[vmem] * len(operands),
        out_specs=vmem,
        scratch_shapes=[
            pltpu.VMEM((2 * BS, NB // N_LAYER * BS), jnp.bfloat16),
            pltpu.VMEM((2 * BS, WIDTH), jnp.float32),
            pltpu.VMEM((16, 128), jnp.int32),
            pltpu.SMEM((16, 128), jnp.int32),
            pltpu.SemaphoreType.DMA,
        ]
        + [pltpu.VMEM((DEPTH, WIDTH), jnp.bfloat16)] * GROUP
        + [pltpu.VMEM((BODY, 128), jnp.bfloat16)] * GROUP,
        compiler_params=pltpu.CompilerParams(vmem_limit_bytes=24 * 1024 * 1024),
        cost_estimate=pl.CostEstimate(
            flops=2 * 128 * 3072 * 2048, bytes_accessed=4 << 20, transcendentals=0
        ),
    )(*operands)


def shards(left_blocks, left_coords, right_blocks, right_coords):
    mine = pack(right_blocks.reshape(SLOTS, BS, BS), right_coords.reshape(SLOTS, 2).T)
    cross = [(0, 1), (1, 0)]
    on = [
        [(2 * i + c, 2 * ((i + d * (1 - 2 * c)) % N_Y) + c) for i in range(N_Y) for c in (0, 1)]
        for d in range(3)
    ]
    axes = ("y", "core")
    both = jnp.stack([mine, lax.ppermute(mine, "core", cross)])
    one = lax.ppermute(both, axes, on[1])
    two = lax.ppermute(both, axes, on[2])
    left = spread(left_blocks.reshape(2, BS, BS), left_coords.reshape(2, 2))
    pieces = lax.all_to_all(left, "col", 0, 0)
    three = lax.ppermute(two, axes, on[1])
    four = lax.ppermute(jnp.where(one[0, BODY, 0] >= 0, two[0], 0), axes, on[2])
    blocks = [mine, one, two, three, four]
    pieces_other = lax.ppermute(pieces, "core", cross)
    part = multiply(pieces, pieces_other, *blocks)
    parts = lax.all_to_all(part, ("core", "layer"), 0, 0)
    total = jnp.sum(parts.astype(jnp.float32), axis=0)
    return total.reshape(1, BS, COLUMNS // N_LAYER, BS)


def solution(mesh):
    grid = Mesh(mesh.devices.reshape(N_Y, 2, N_COL, N_LAYER), ("y", "core", "col", "layer"))
    row = ("y", "core")
    return jax.shard_map(
        shards,
        mesh=grid,
        in_specs=(
            P(row, "col", "layer", None, None, None),
            P(row, "col", "layer", None, None),
            P(row, "col", "layer", None, None, None),
            P(row, "col", "layer", None, None),
        ),
        out_specs=P(row, None, ("col", "layer"), None),
        check_vma=False,
    )
```
